256 devices in a mesh: space: 16 (over z, y_hi), leaf: 16 (over x, y_lo, core).
Axes of the slice: x: 4, y: 4 (y_hi: 2, y_lo: 2; y = y_hi * 2 + y_lo), z: 8, core: 2. Of those that a mesh axis runs over, the one named last changes fastest.
Arguments:
- charges: bfloat16 [16, 2097152], P(None, ('space', 'leaf')), may hold values from -6 to 6
- leaf_basis: bfloat16 [16384, 64, 128], P(('space', 'leaf')), may hold values from -0.5 to 0.5
- transfer_one: bfloat16 [2048, 64, 512], P(('space', 'leaf')), may hold values from -0.25 to 0.25
- transfer_two: bfloat16 [256, 64, 512], P(('space', 'leaf')), may hold values from -0.25 to 0.25
- nodes_leaf: bfloat16 [16384, 3, 64], P(('space', 'leaf')), may hold values from 0 to 6
- nodes_one: bfloat16 [2048, 3, 64], P(('space', 'leaf')), may hold values from 0 to 6
- nodes_two: bfloat16 [256, 3, 64], P(('space', 'leaf')), may hold values from 0 to 6
- links_leaf: int32 [16384, 96], P(('space', 'leaf')), may hold values from -1 to 16383, as said below
- links_one: int32 [2048, 96], P(('space', 'leaf')), may hold values from -1 to 2047, as said below
- links_two: int32 [256, 96], P(('space', 'leaf')), may hold values from -1 to 255, as said below
Outputs:
- potentials: bfloat16 [16, 2097152], P(None, ('space', 'leaf'))
The draws below stay inside these ranges and needn't reach their ends.
Inputs may be any that keep to these rules, and one draw needn't show every extreme that they name: `links_leaf`: A live source leaf lies on a device whose space index differs from that of the target leaf's device by at most one; live slots of a row come first. `links_one`: A live source cluster lies on a device whose space index differs from that of the target's device by at most one; live slots of a row come first. `links_two`: live slots of a row come first.
All inputs are finite; a program needn't handle non-finite values.
Results may differ from the reference program's by a relative error of at most 0.007.
Values may be sent and summed in bfloat16 or wider, within the bound.
A program may use at most 128 MiB of HBM per device.

```python
import jax
import jax.numpy as jnp
from jax import lax

NV = 16
LEAF = 128
K = 64
SLOTS = 96
LEAF_DEV = 64
LEAVES = 16384
POINTS = 2097152
CLUSTERS_ONE = 2048
CLUSTERS_TWO = 256
N_SPACE = 16
N_LEAF = 16


def make_links(key, targets, per_dev, reach):
    keys = jax.random.split(key, 5)
    target_ids = jnp.arange(targets, dtype=jnp.int32)
    device = target_ids // per_dev
    space_id = device // N_LEAF
    step_space = jax.random.randint(keys[0], (targets, SLOTS), -1, 2)
    if reach == 1:
        src_space = jnp.clip(space_id[:, None] + step_space, 0, N_SPACE - 1)
        src_leaf = jax.random.randint(keys[1], (targets, SLOTS), 0, N_LEAF)
    else:
        src_space = jax.random.randint(keys[0], (targets, SLOTS), 0, N_SPACE)
        src_leaf = jax.random.randint(keys[1], (targets, SLOTS), 0, N_LEAF)
    local = jax.random.randint(keys[2], (targets, SLOTS), 0, per_dev)
    source = (src_space * N_LEAF + src_leaf) * per_dev + local
    device_count = jax.random.randint(keys[3], (N_SPACE * N_LEAF,), SLOTS // 2, SLOTS + 1)
    lower = jax.random.randint(keys[4], (targets,), 0, SLOTS // 8 + 1)
    count = jnp.maximum(device_count[device] - lower, 1)
    count = count.at[0].set(1)
    live = jnp.arange(SLOTS, dtype=jnp.int32)[None, :] < count[:, None]
    source = jnp.where(live, source, -1)
    source = source.at[targets - 2, 0].set(targets - 1)
    return source.astype(jnp.int32)


def draw_links_leaf(key, part):
    return make_links(jax.random.fold_in(key, 11), LEAVES, LEAF_DEV, 1)


def draw_links_one(key, part):
    return make_links(jax.random.fold_in(key, 12), CLUSTERS_ONE, LEAF_DEV // 8, 1)


def draw_links_two(key, part):
    return make_links(jax.random.fold_in(key, 13), CLUSTERS_TWO, LEAF_DEV // 64, 2)


def steps_of(stream_key, shape, cuts, low, largest):
    def one(axis_at, parts):
        steps = jax.random.uniform(jax.random.fold_in(jax.random.fold_in(stream_key, 6), axis_at), (parts,), jnp.float32, low / len(cuts), largest / len(cuts))
        return jnp.repeat(jnp.exp(steps), shape[axis_at] // parts).reshape((-1,) + (1,) * (len(shape) - axis_at - 1))

    factor_of = one(*cuts[0])
    for cut in cuts[1:]:
        factor_of = factor_of * one(*cut)
    return factor_of


def bell_draw(key, shape, deviation, bound, cuts=(), kind=jnp.bfloat16):
    values = jax.random.normal(key, shape, jnp.float32) * deviation
    if len(cuts) > 0:
        values = steps_of(key, shape, cuts, -0.22, 0.18) * values
    return jnp.clip(values, min=-bound, max=bound).astype(kind)


def setup_inputs(seed: int = 0) -> dict:
    seeds = jax.random.split(jax.random.key(seed), 11)
    return {
        "charges": bell_draw(seeds[0], (NV, POINTS), 1.0, 6.0, ((1, 256),)),
        "leaf_basis": bell_draw(seeds[1], (LEAVES, K, LEAF), LEAF ** -0.5, 0.5, ((0, 256),)),
        "transfer_one": bell_draw(seeds[2], (CLUSTERS_ONE, K, 8 * K), (8 * K) ** -0.5, 0.25, ((0, 256),)),
        "transfer_two": bell_draw(seeds[3], (CLUSTERS_TWO, K, 8 * K), (8 * K) ** -0.5, 0.25, ((0, 256),)),
        "nodes_leaf": jnp.clip(6.0 * jax.random.uniform(seeds[4], (LEAVES, 3, K), jnp.float32) ** steps_of(seeds[4], (LEAVES, 3, K), ((0, 256),), -0.2, 0.2), 0.0, 6.0).astype(jnp.bfloat16),
        "nodes_one": jnp.clip(6.0 * jax.random.uniform(seeds[5], (CLUSTERS_ONE, 3, K), jnp.float32) ** steps_of(seeds[5], (CLUSTERS_ONE, 3, K), ((0, 256),), -0.2, 0.2), 0.0, 6.0).astype(jnp.bfloat16),
        "nodes_two": jnp.clip(6.0 * jax.random.uniform(seeds[6], (CLUSTERS_TWO, 3, K), jnp.float32) ** steps_of(seeds[6], (CLUSTERS_TWO, 3, K), ((0, 256),), -0.2, 0.2), 0.0, 6.0).astype(jnp.bfloat16),
        "links_leaf": draw_links_leaf(jax.random.fold_in(seeds[10], 71), 0),
        "links_one": draw_links_one(jax.random.fold_in(seeds[10], 71), 0),
        "links_two": draw_links_two(jax.random.fold_in(seeds[10], 71), 0),
    }


SQRT_THREE = 1.7320508075688772
LENGTH = 2.0
AMPLITUDE = 0.25

def matern_block(target_nodes, source_nodes):
    diff = target_nodes[:, None, :, :, None] - source_nodes[:, :, :, None, :]
    dist = jnp.sqrt(lax.optimization_barrier(jnp.sum(diff * diff, axis=2))) * (SQRT_THREE / LENGTH)
    return (AMPLITUDE * (1.0 + dist) * jnp.exp(-dist)).astype(jnp.bfloat16)

def couple(coeffs, nodes, links, target_nodes, group):
    count = links.shape[0]
    slots = links.shape[1]
    rank = coeffs.shape[1]
    width = coeffs.shape[2]
    live = links >= 0
    safe = jnp.where(live, links, 0).astype(jnp.int32)

    def one_group(args):
        index, alive, tnodes = args
        picked = jnp.where(alive[:, :, None, None], coeffs[index], jnp.zeros((), jnp.bfloat16))
        source_nodes = nodes[index].astype(jnp.float32)
        matrix = matern_block(tnodes.astype(jnp.float32), source_nodes)
        return jnp.einsum('gjab,gjbv->gav', matrix.astype(jnp.float32), picked.astype(jnp.float32))
    result = lax.map(one_group, (safe.reshape(-1, group, slots), live.reshape(-1, group, slots), target_nodes.reshape(-1, group, 3, rank)))
    return result.reshape(count, rank, width)

def reference(charges, leaf_basis, transfer_one, transfer_two, nodes_leaf, nodes_one, nodes_two, links_leaf, links_one, links_two):
    leaves = leaf_basis.shape[0]
    rank = leaf_basis.shape[1]
    leaf_size = leaf_basis.shape[2]
    width = charges.shape[0]
    shaped = charges.reshape(width, leaves, leaf_size)
    coef_leaf = jnp.einsum('tkp,vtp->tkv', leaf_basis.astype(jnp.float32), shaped.astype(jnp.float32)).astype(jnp.bfloat16)
    count_one = leaves // 8
    count_two = leaves // 64
    coef_one = jnp.einsum('pkm,pmv->pkv', transfer_one.astype(jnp.float32), coef_leaf.reshape(count_one, 8 * rank, width).astype(jnp.float32)).astype(jnp.bfloat16)
    coef_two = jnp.einsum('pkm,pmv->pkv', transfer_two.astype(jnp.float32), coef_one.reshape(count_two, 8 * rank, width).astype(jnp.float32)).astype(jnp.bfloat16)
    far_leaf = couple(coef_leaf, nodes_leaf, links_leaf, nodes_leaf, 16)
    far_one = couple(coef_one, nodes_one, links_one, nodes_one, 8)
    far_two = couple(coef_two, nodes_two, links_two, nodes_two, 1)
    local_two = far_two.astype(jnp.bfloat16)
    down_one = jnp.einsum('pkm,pkv->pmv', transfer_two.astype(jnp.float32), local_two.astype(jnp.float32))
    local_one = (far_one + down_one.reshape(count_one, rank, width)).astype(jnp.bfloat16)
    down_leaf = jnp.einsum('pkm,pkv->pmv', transfer_one.astype(jnp.float32), local_one.astype(jnp.float32))
    local_leaf = (far_leaf + down_leaf.reshape(leaves, rank, width)).astype(jnp.bfloat16)
    result = jnp.einsum('tkp,tkv->vtp', leaf_basis.astype(jnp.float32), local_leaf.astype(jnp.float32))
    return result.reshape(width, leaves * leaf_size).astype(jnp.bfloat16)
```

```python
import functools

import jax
import jax.numpy as jnp
from jax import lax
from jax.experimental import pallas as pl
from jax.experimental.pallas import tpu as pltpu
from jax.sharding import PartitionSpec as P

SCALE = 1.7320508075688772 / 2.0
AMPLITUDE = 0.25
LOG2E = 1.4426950408889634
MESH = pl.DeviceIdType.MESH
F32 = jnp.float32
BF16 = jnp.bfloat16

RANK = 64
LEAF_DEV = 64
ONE_DEV = 8
PAIRS = 37
PLANE = 48
ROWS = 80
SLOT = 72
TWO_AT = 12 * SLOT
ZERO_AT = TWO_AT + 64
ENTRIES = ZERO_AT + 8
UNROLL = 32

DIRECT = ((0, 1), (1, 0), (1, 1), (-1, 0), (-1, 1))


def nt(a, b):
    return lax.dot_general(a, b, (((1,), (1,)), ((), ())), preferred_element_type=F32)


def split3(value):
    first = value.astype(BF16).astype(F32)
    rest = value - first
    second = rest.astype(BF16).astype(F32)
    return first, second, rest - second


def up_kernel(
    n_space,
    charges, basis, t_one, t_two, nodes, links,
    node_tab, coef_tab, two_tab, target_nodes, lists,
    coef, entry, packed, order, value,
    local_sem, send_n, send_c, send_o, recv_n, recv_c, recv_o,
    send_e, recv_e, send_b, recv_b, send_x, recv_x, send_l, recv_l,
):
    space = lax.axis_index("space")
    leaf = lax.axis_index("leaf")
    x = leaf // 4
    four = lax.rem(leaf, 4)
    y_lo = four // 2
    core = lax.rem(four, 2)
    other_y = x * 4 + (1 - y_lo) * 2 + core
    sibling = x * 4 + y_lo * 2 + (1 - core)
    four_y = (1 - y_lo) * 2 + core
    has_prev = space > 0
    has_next = space < n_space - 1

    barrier = pltpu.get_barrier_semaphore()

    def greet(s, l):
        pl.semaphore_signal(barrier, inc=1, device_id=(s, l), device_id_type=MESH)

    for k in range(1, 4):
        greet(space, lax.rem(x + k, 4) * 4 + four)
    for k in range(1, n_space):
        greet(lax.rem(space + k, n_space), leaf)
    greet(space, other_y)
    greet(space, sibling)

    @pl.when(has_next)
    def _():
        greet(space + 1, other_y)

    @pl.when(has_prev)
    def _():
        greet(space - 1, other_y)

    def leaves(i, carry):
        for j in range(4):
            pair = i * 4 + j
            halves = [
                nt(charges[:, pl.ds(pl.multiple_of((2 * pair + h) * 128, 128), 128)], basis[2 * pair + h])
                for h in range(2)
            ]
            coef[pair] = jnp.concatenate(halves, axis=1).astype(BF16)
        return carry

    lax.fori_loop(0, 8, leaves, 0)

    neighbours = has_prev.astype(jnp.int32) + has_next.astype(jnp.int32)
    pl.semaphore_wait(barrier, 3 + (n_space - 1) + 2 + neighbours)

    def guarded(delta):
        if delta == 0:
            return lambda f: f()
        return pl.when(has_next if delta > 0 else has_prev)

    def remote(src, dst, send, recv, s, l):
        return pltpu.make_async_remote_copy(
            src_ref=src, dst_ref=dst, send_sem=send, recv_sem=recv, device_id=(s, l), device_id_type=MESH
        )

    LEAF_PART = pl.ds(0, 32)
    ONE_PART = pl.ds(32, 4)
    mine = 4 + four

    def node_copy(src, slot, k, s, l):
        return remote(src, node_tab.at[slot], send_n.at[k], recv_n.at[slot], s, l)

    def leaf_copy(src, slot, k, s, l):
        return remote(src, coef_tab.at[slot, LEAF_PART], send_c.at[k], recv_c.at[slot], s, l)

    def one_copy(src, slot, k, s, l):
        return remote(src, coef_tab.at[slot, ONE_PART], send_o.at[k], recv_o.at[slot], s, l)

    def place(delta, flip):
        return space + delta, (other_y if flip else leaf)

    def direct(make, src):
        for k, (delta, flip) in enumerate(DIRECT):
            @guarded(delta)
            def _(k=k, delta=delta, flip=flip):
                make(src, (1 - delta) * 4 + four, k, *place(delta, flip)).start()
        make(src, mine, 5, space, sibling).start()

    direct(leaf_copy, coef.at[LEAF_PART])
    direct(node_copy, nodes)
    for k in range(1, 4):
        to = lax.rem(x + k, 4) * 4 + four
        remote(nodes, target_nodes.at[x], send_x.at[k], recv_x.at[x], space, to).start()

    for i in range(4):
        halves = []
        for h in range(2):
            p = 2 * i + h
            stacked = jnp.concatenate([coef[4 * p + j] for j in range(4)], axis=1)
            halves.append(nt(stacked, t_one[p]))
        coef[32 + i] = jnp.concatenate(halves, axis=1).astype(BF16)
    direct(one_copy, coef.at[ONE_PART])

    top = nt(jnp.concatenate([coef[32 + j] for j in range(4)], axis=1), t_two[0])
    tile = nodes[32:48].astype(F32), nodes[80:96].astype(F32), nodes[128:144].astype(F32)
    tx, ty, tz = (part[4:5, :RANK] for part in tile)
    parts = (tx, ty, tz) + split3(tx * tx + ty * ty + tz * tz)
    row = lax.broadcasted_iota(jnp.int32, (16, RANK), 0)
    feature = jnp.where((row >= 6) & (row < 9), 1.0, 0.0)
    for k, part in enumerate(parts):
        feature = jnp.where(row == k, jnp.broadcast_to(part, (16, RANK)), feature)
    entry[...] = jnp.concatenate([feature, top], axis=1).astype(BF16)

    own_two = four * n_space + space

    def two_copy(k):
        return remote(
            entry, two_tab.at[own_two], send_e.at[k], recv_e.at[space],
            lax.rem(space + k, n_space), leaf,
        )

    for k in range(1, n_space):
        two_copy(k).start()
    keep_two = pltpu.make_async_copy(entry, two_tab.at[own_two], local_sem.at[0])
    keep_two.start()

    keeps = [
        pltpu.make_async_copy(nodes, node_tab.at[mine], local_sem.at[1]),
        pltpu.make_async_copy(coef.at[pl.ds(0, 36)], coef_tab.at[mine], local_sem.at[2]),
        pltpu.make_async_copy(nodes, target_nodes.at[x], local_sem.at[3]),
    ]
    for keep in keeps:
        keep.start()

    code = links[...]
    group = code // 1024
    entry_of = code - group * 1024
    before = jnp.where(
        lax.broadcasted_iota(jnp.int32, (128, 128), 0) < lax.broadcasted_iota(jnp.int32, (128, 128), 1), 1.0, 0.0
    ).astype(BF16)
    at = jnp.full((ROWS, 128), -1.0, F32)
    counts = []
    for q in range(4):
        member = jnp.where(group == q, 1.0, 0.0)
        rank = jnp.dot(member.astype(BF16), before, preferred_element_type=F32)
        at = jnp.where(group == q, rank + 128.0 * q, at)
        counts.append(jnp.sum(member, axis=1, keepdims=True))
    order[...] = at
    value[...] = entry_of.astype(F32)
    lane = lax.broadcasted_iota(jnp.int32, (8, 128), 1)
    lane_f = lane.astype(F32)
    for q in range(4):
        packed[q] = jnp.broadcast_to(jnp.maximum((counts[q].astype(jnp.int32) + 3) // 4, 1), (ROWS, 128))

    def compact(b, carry):
        rows = pl.ds(pl.multiple_of(b * 8, 8), 8)
        where = order[rows, :]
        what = value[rows, :]
        found = [jnp.full((8, 128), float(ZERO_AT), F32) for _ in range(4)]
        for j in range(96):
            w = jnp.broadcast_to(where[:, j : j + 1], (8, 128))
            v = jnp.broadcast_to(what[:, j : j + 1], (8, 128))
            for q in range(4):
                found[q] = jnp.where(w == lane_f + 128.0 * q, v, found[q])
        for q in range(4):
            packed[q, rows, :] = jnp.where(lane == 127, packed[q, rows, :], found[q].astype(jnp.int32))
        return carry

    lax.fori_loop(0, ROWS // 8, compact, 0)
    for k in range(1, 4):
        to = lax.rem(x + k, 4)
        remote(packed.at[to], lists.at[x], send_l.at[k], recv_l.at[x], space, to * 4 + four).start()
    keep_list = pltpu.make_async_copy(packed.at[x], lists.at[x], local_sem.at[4])
    keep_list.start()

    def hand_on(make, table, part):
        for k, (delta, flip) in enumerate(DIRECT):
            @guarded(delta)
            def _(k=k, delta=delta, flip=flip):
                slot = (1 + delta) * 4 + (four_y if flip else four)
                source = table.at[slot] if part is None else table.at[slot, part]
                make(source, slot, k, space, leaf).wait_recv()
                make(source, slot, 6 + k, space, sibling).start()

    hand_on(node_copy, node_tab, None)

    for k in range(1, n_space):
        source = lax.rem(space + k, n_space)
        remote(
            entry, two_tab.at[four * n_space + source], send_e.at[0], recv_e.at[source], space, leaf
        ).wait_recv()
    keep_two.wait()

    def band(which):
        return two_tab.at[pl.ds(which * n_space, n_space)]

    remote(band(four), band(four), send_b.at[0], recv_b.at[four], space, other_y).start()
    remote(band(four), band(four), send_b.at[1], recv_b.at[four], space, sibling).start()

    hand_on(leaf_copy, coef_tab, LEAF_PART)
    hand_on(one_copy, coef_tab, ONE_PART)

    remote(band(four_y), band(four_y), send_b.at[0], recv_b.at[four_y], space, other_y).wait_recv()
    remote(band(four_y), band(four_y), send_b.at[2], recv_b.at[four_y], space, sibling).start()

    beside = y_lo * 2 + (1 - core)
    beside_y = (1 - y_lo) * 2 + (1 - core)

    def last(make, table, part):
        for delta, flip in ((0, 0),) + DIRECT:
            @guarded(delta)
            def _(delta=delta, flip=flip):
                slot = (1 + delta) * 4 + (beside_y if flip else beside)
                source = table.at[slot] if part is None else table.at[slot, part]
                make(source, slot, 5, space, sibling).wait_recv()

    last(node_copy, node_tab, None)
    last(leaf_copy, coef_tab, LEAF_PART)
    last(one_copy, coef_tab, ONE_PART)
    for which in (beside, beside_y):
        remote(band(which), band(which), send_b.at[1], recv_b.at[which], space, sibling).wait_recv()
    for k in range(1, 4):
        source = lax.rem(x + k, 4)
        remote(nodes, target_nodes.at[source], send_x.at[k], recv_x.at[source], space, leaf).wait_recv()
        remote(packed.at[0], lists.at[source], send_l.at[k], recv_l.at[source], space, leaf).wait_recv()

    def sent(make, src, table, part):
        for k, (delta, flip) in enumerate(DIRECT):
            @guarded(delta)
            def _(k=k, delta=delta, flip=flip):
                make(src, (1 - delta) * 4 + four, k, *place(delta, flip)).wait_send()
                slot = (1 + delta) * 4 + (four_y if flip else four)
                source = table.at[slot] if part is None else table.at[slot, part]
                make(source, slot, 6 + k, space, sibling).wait_send()
        make(src, mine, 5, space, sibling).wait_send()

    sent(node_copy, nodes, node_tab, None)
    sent(leaf_copy, coef.at[LEAF_PART], coef_tab, LEAF_PART)
    sent(one_copy, coef.at[ONE_PART], coef_tab, ONE_PART)
    for k in range(1, n_space):
        two_copy(k).wait_send()
    remote(band(four), band(four), send_b.at[0], recv_b.at[four], space, other_y).wait_send()
    remote(band(four), band(four), send_b.at[1], recv_b.at[four], space, sibling).wait_send()
    remote(band(four_y), band(four_y), send_b.at[2], recv_b.at[four_y], space, sibling).wait_send()
    for k in range(1, 4):
        to = lax.rem(x + k, 4)
        remote(nodes, target_nodes.at[x], send_x.at[k], recv_x.at[x], space, to * 4 + four).wait_send()
        remote(packed.at[to], lists.at[x], send_l.at[k], recv_l.at[x], space, to * 4 + four).wait_send()
    for keep in keeps:
        keep.wait()
    keep_list.wait()


def upward(n_space, charges, basis, t_one, t_two, nodes, links):
    vmem = pl.BlockSpec(memory_space=pltpu.VMEM)
    hbm = pl.BlockSpec(memory_space=pl.ANY)
    dma = pltpu.SemaphoreType.DMA
    return pl.pallas_call(
        functools.partial(up_kernel, n_space),
        out_shape=(
            jax.ShapeDtypeStruct((12, 3 * PLANE, 128), BF16),
            jax.ShapeDtypeStruct((12, 36, 16, 128), BF16),
            jax.ShapeDtypeStruct((64, 16, 128), BF16),
            jax.ShapeDtypeStruct((4, 3 * PLANE, 128), BF16),
            jax.ShapeDtypeStruct((4, ROWS, 128), jnp.int32),
        ),
        in_specs=[vmem] * 6,
        out_specs=[hbm] * 5,
        scratch_shapes=[
            pltpu.VMEM((PAIRS, 16, 128), BF16),
            pltpu.VMEM((16, 128), BF16),
            pltpu.VMEM((4, ROWS, 128), jnp.int32),
            pltpu.VMEM((ROWS, 128), F32),
            pltpu.VMEM((ROWS, 128), F32),
            dma((5,)),
            dma((11,)), dma((11,)), dma((11,)),
            dma((12,)), dma((12,)), dma((12,)),
            dma((16,)), dma((16,)),
            dma((3,)), dma((4,)),
            dma((4,)), dma((4,)),
            dma((4,)), dma((4,)),
        ],
        compiler_params=pltpu.CompilerParams(
            collective_id=0, has_side_effects=True, vmem_limit_bytes=24 * 1024 * 1024
        ),
        name="upward",
    )(charges, basis, t_one, t_two, nodes, links)


def couple_kernel(
    lists, node_tab, coef_tab, two_tab, target_nodes, out, table, targets, total, feat
):
    def fill(planes, base, sources):
        px, py, pz = (planes[base, pl.ds(c * PLANE, PLANE), :].astype(F32) for c in range(3))
        norm = split3(px * px + py * py + pz * pz)
        ones = jnp.ones((PLANE, 128), F32)
        zeros = jnp.zeros((PLANE, 128), F32)
        if sources:
            parts = (px, py, pz) + norm + (ones,) * 3
        else:
            parts = (-2.0 * px, -2.0 * py, -2.0 * pz) + (ones,) * 3 + norm
        for k, part in enumerate(parts):
            feat[pl.ds(k, PLANE, stride=16), :] = part

    zeros = jnp.zeros((PLANE, 128), F32)
    for k in range(9, 16):
        feat[pl.ds(k, PLANE, stride=16), :] = zeros

    def one_source(slot, carry):
        fill(node_tab, slot, True)
        for i in range(36):
            f = feat[16 * i : 16 * i + 16, :].astype(BF16)
            c = coef_tab[slot, i]
            table[slot * SLOT + 2 * i] = jnp.concatenate([f[:, :RANK], c[:, :RANK]], axis=1)
            table[slot * SLOT + 2 * i + 1] = jnp.concatenate([f[:, RANK:], c[:, RANK:]], axis=1)
        return carry

    lax.fori_loop(0, 12, one_source, 0)
    table[pl.ds(TWO_AT, 64)] = two_tab[...]
    table[ZERO_AT] = jnp.zeros((16, 128), BF16)

    def one_target(slot, carry):
        fill(target_nodes, slot, False)
        for i in range(40):
            f = feat[16 * i : 16 * i + 16, :]
            start = pl.multiple_of(slot * (ROWS * RANK) + i * 128, 128)
            targets[pl.ds(start, 128), :] = f.T.astype(BF16)
        return carry

    lax.fori_loop(0, 4, one_target, 0)

    def clear(i, carry):
        for j in range(16):
            total[i * 16 + j] = jnp.zeros((16, RANK), F32)
        return carry

    lax.fori_loop(0, 4 * ROWS // 16, clear, 0)

    end = 4 * ROWS - 1

    def step(carry):
        r, t, g = carry
        for _ in range(UNROLL):
            picked = [table[lists[r, 4 * g + i]] for i in range(4)]
            sources = jnp.concatenate([e[:, :RANK] for e in picked], axis=1)
            coefs = jnp.concatenate([e[:, RANK:] for e in picked], axis=1)
            mine = targets[pl.ds(pl.multiple_of(r * RANK, RANK), RANK), :]
            square = jnp.maximum(jnp.dot(mine, sources, preferred_element_type=F32), 1e-20)
            dist = square * lax.rsqrt(square)
            matrix = ((dist + 1.0 / SCALE) * jnp.exp2(dist * (-SCALE * LOG2E))).astype(BF16)
            total[r] += nt(coefs, matrix)
            done = g + 1 >= lists[r, 127]
            over = t == 72
            r = jnp.where(done, jnp.minimum(jnp.where(over, r + 8, r + 1), end), r)
            t = jnp.where(done, jnp.where(over, 0, t + 1), t)
            g = jnp.where(done, 0, g + 1)
        return r, t, g

    lax.while_loop(lambda c: c[0] < end, step, (jnp.int32(0), jnp.int32(0), jnp.int32(0)))

    def pack(i, carry):
        for q in range(4):
            at = q * ROWS + 2 * i
            both = jnp.concatenate([total[at], total[at + 1]], axis=1)
            out[q, i] = (both * (AMPLITUDE * SCALE)).astype(BF16)
        return carry

    lax.fori_loop(0, PAIRS, pack, 0)


def coupling(lists, node_tab, coef_tab, two_tab, target_nodes):
    vmem = pl.BlockSpec(memory_space=pltpu.VMEM)
    return pl.pallas_call(
        couple_kernel,
        grid_spec=pltpu.PrefetchScalarGridSpec(
            num_scalar_prefetch=1,
            grid=(),
            in_specs=[vmem] * 4,
            out_specs=vmem,
            scratch_shapes=[
                pltpu.VMEM((ENTRIES, 16, 128), BF16),
                pltpu.VMEM((4 * ROWS * RANK, 16), BF16),
                pltpu.VMEM((4 * ROWS, 16, RANK), F32),
                pltpu.VMEM((PLANE * 16, 128), F32),
            ],
        ),
        out_shape=jax.ShapeDtypeStruct((4, PAIRS, 16, 128), BF16),
        compiler_params=pltpu.CompilerParams(vmem_limit_bytes=40 * 1024 * 1024),
        name="coupling",
    )(lists, node_tab, coef_tab, two_tab, target_nodes)


def down_kernel(far, basis, t_one, t_two, out, came, near, send, recv):
    space = lax.axis_index("space")
    leaf = lax.axis_index("leaf")
    x = leaf // 4
    four = lax.rem(leaf, 4)
    barrier = pltpu.get_barrier_semaphore()
    for k in range(1, 4):
        to = lax.rem(x + k, 4) * 4 + four
        pl.semaphore_signal(barrier, inc=1, device_id=(space, to), device_id_type=MESH)
    pl.semaphore_wait(barrier, 3)

    def copy(k):
        to = lax.rem(x + k, 4)
        return pltpu.make_async_remote_copy(
            src_ref=far.at[to], dst_ref=came.at[x], send_sem=send.at[k], recv_sem=recv.at[x],
            device_id=(space, to * 4 + four), device_id_type=MESH,
        )

    for k in range(1, 4):
        copy(k).start()
    came[x] = far[x]
    for k in range(1, 4):
        source = lax.rem(x + k, 4)
        pltpu.make_async_remote_copy(
            src_ref=far.at[source], dst_ref=came.at[source], send_sem=send.at[k], recv_sem=recv.at[source],
            device_id=(space, leaf), device_id_type=MESH,
        ).wait_recv()

    def summed(i):
        return (
            came[0, i].astype(F32) + came[1, i].astype(F32)
            + came[2, i].astype(F32) + came[3, i].astype(F32)
        )

    local_two = summed(36)[:, :RANK].astype(BF16)
    down_one = jnp.dot(local_two, t_two[0], preferred_element_type=F32)
    for i in range(4):
        near[32 + i] = (summed(32 + i) + down_one[:, 128 * i : 128 * i + 128]).astype(BF16)

    def cluster(i, carry):
        both = near[32 + i]
        for h in range(2):
            local_one = both[:, h * RANK : (h + 1) * RANK]
            down_leaf = jnp.dot(local_one, t_one[2 * i + h], preferred_element_type=F32)
            for j in range(4):
                pair = 8 * i + 4 * h + j
                local_leaf = (summed(pair) + down_leaf[:, 128 * j : 128 * j + 128]).astype(BF16)
                for s in range(2):
                    at = pl.multiple_of((2 * pair + s) * 128, 128)
                    out[:, pl.ds(at, 128)] = jnp.dot(
                        local_leaf[:, s * RANK : (s + 1) * RANK], basis[2 * pair + s],
                        preferred_element_type=F32,
                    ).astype(BF16)
        return carry

    lax.fori_loop(0, 4, cluster, 0)
    for k in range(1, 4):
        copy(k).wait_send()


def downward(far, basis, t_one, t_two):
    vmem = pl.BlockSpec(memory_space=pltpu.VMEM)
    dma = pltpu.SemaphoreType.DMA
    return pl.pallas_call(
        down_kernel,
        out_shape=jax.ShapeDtypeStruct((16, LEAF_DEV * 128), BF16),
        in_specs=[vmem] * 4,
        out_specs=vmem,
        scratch_shapes=[
            pltpu.VMEM((4, PAIRS, 16, 128), BF16),
            pltpu.VMEM((36, 16, 128), BF16),
            dma((4,)), dma((4,)),
        ],
        compiler_params=pltpu.CompilerParams(
            collective_id=1, has_side_effects=True, vmem_limit_bytes=24 * 1024 * 1024
        ),
        name="downward",
    )(far, basis, t_one, t_two)


def packed_nodes(*levels):
    rows = []
    for nodes in levels:
        flat = nodes.transpose(1, 0, 2).reshape(3, -1)
        flat = jnp.pad(flat, ((0, 0), (0, -flat.shape[1] % 128)))
        rows.append(flat.reshape(3, -1, 128))
    whole = jnp.concatenate(rows, axis=1)
    whole = jnp.pad(whole, ((0, 0), (0, PLANE - whole.shape[1]), (0, 0)))
    return whole.reshape(3 * PLANE, 128)


def coded_links(links_leaf, links_one, links_two, space):
    def near(links, per_dev, offset):
        owner = links // per_dev
        slot = (owner // 16 - space + 1) * 4 + owner % 4
        return owner // 4 % 4 * 1024 + slot * SLOT + offset + links % per_dev

    two = links_two // 4 % 4 * 1024 + TWO_AT + links_two % 4 * 16 + links_two // 16
    links = jnp.concatenate([links_leaf, links_one, links_two], axis=0)
    codes = jnp.concatenate(
        [near(links_leaf, LEAF_DEV, 0), near(links_one, ONE_DEV, LEAF_DEV), two], axis=0
    )
    codes = jnp.where(links >= 0, codes, 4096)
    rows, slots = codes.shape
    return jnp.pad(codes, ((0, ROWS - rows), (0, 128 - slots)), constant_values=4096)


def local(
    charges, leaf_basis, transfer_one, transfer_two, nodes_leaf, nodes_one, nodes_two,
    links_leaf, links_one, links_two,
):
    n_space = lax.axis_size("space")
    nodes = packed_nodes(nodes_leaf, nodes_one, nodes_two)
    links = coded_links(links_leaf, links_one, links_two, lax.axis_index("space"))
    node_tab, coef_tab, two_tab, target_nodes, lists = upward(
        n_space, charges, leaf_basis, transfer_one, transfer_two, nodes, links
    )
    far = coupling(lists.reshape(4 * ROWS, 128), node_tab, coef_tab, two_tab, target_nodes)
    return downward(far, leaf_basis, transfer_one, transfer_two)


def solution(mesh):
    return jax.shard_map(
        local,
        mesh=mesh,
        in_specs=(
            P(None, ("space", "leaf")),
            P(("space", "leaf"), None, None),
            P(("space", "leaf"), None, None),
            P(("space", "leaf"), None, None),
            P(("space", "leaf"), None, None),
            P(("space", "leaf"), None, None),
            P(("space", "leaf"), None, None),
            P(("space", "leaf"), None),
            P(("space", "leaf"), None),
            P(("space", "leaf"), None),
        ),
        out_specs=P(None, ("space", "leaf")),
        check_vma=False,
    )
```

```python
import functools

import jax
import jax.numpy as jnp
from jax import lax
from jax.experimental import pallas as pl
from jax.experimental.pallas import tpu as pltpu
from jax.sharding import PartitionSpec as P

SCALE = 1.7320508075688772 / 2.0
AMPLITUDE = 0.25
LOG2E = 1.4426950408889634
MESH = pl.DeviceIdType.MESH
F32 = jnp.float32
BF16 = jnp.bfloat16

RANK = 64
LEAF_DEV = 64
ONE_DEV = 8
PAIRS = 37
PLANE = 48
ROWS = 80
SLOT = 72
TWO_AT = 12 * SLOT
ZERO_AT = TWO_AT + 64
ENTRIES = ZERO_AT + 8
UNROLL = 96

PIECES = 3
CUT = 16
BLOCKS = 5
VMEM_BYTES = 58 * 1024 * 1024


def nt(a, b):
    return lax.dot_general(a, b, (((1,), (1,)), ((), ())), preferred_element_type=F32)


def split3(value):
    first = value.astype(BF16).astype(F32)
    rest = value - first
    second = rest.astype(BF16).astype(F32)
    return first, second, rest - second


def up_kernel(
    n_space,
    charges_in, basis_in, t_one_in, t_two_in, leaf_nodes_in, one_nodes_in, two_nodes_in,
    leaf_links_in, one_links_in, two_links_in,
    table_out, blocks_out, lists,
    charges, basis, t_one, t_two, leaf_nodes, one_nodes, two_nodes, leaf_links, one_links, two_links,
    nodes_f, nodes, coef, entry, packed, order, value, feat, feat_t,
    node_tab, coef_tab, two_tab, target_nodes, table, blocks,
    in_sem, out_sem, local_sem, send_own, send_relay, send_z, send_sib, recv,
    send_e, recv_e, send_b, recv_b, send_x, recv_x, send_l, recv_l,
):
    space = lax.axis_index("space")
    leaf = lax.axis_index("leaf")
    x = leaf // 4
    four = lax.rem(leaf, 4)
    y_lo = four // 2
    core = lax.rem(four, 2)
    four_y = (1 - y_lo) * 2 + core
    beside = y_lo * 2 + (1 - core)
    beside_y = (1 - y_lo) * 2 + (1 - core)
    other_y = x * 4 + four_y
    sibling = x * 4 + beside
    side = 1 - 2 * lax.rem(space, 2)
    plane = space + side
    ahead = space + 2 * side
    behind = space - 2 * side
    has_ahead = (ahead >= 0) & (ahead < n_space)
    has_behind = (behind >= 0) & (behind < n_space)
    near, far = (1 + side) * 4, (1 - side) * 4

    loads = [
        pltpu.make_async_copy(src, dst, in_sem.at[k])
        for k, (src, dst) in enumerate(
            (
                (leaf_nodes_in, leaf_nodes), (one_nodes_in, one_nodes), (two_nodes_in, two_nodes),
                (charges_in, charges), (basis_in, basis), (t_one_in, t_one), (t_two_in, t_two),
                (leaf_links_in, leaf_links), (one_links_in, one_links), (two_links_in, two_links),
            )
        )
    ]
    for load in loads:
        load.start()

    barrier = pltpu.get_barrier_semaphore()

    def greet(s, l):
        pl.semaphore_signal(barrier, inc=1, device_id=(s, l), device_id_type=MESH)

    for k in range(1, 4):
        greet(space, lax.rem(x + k, 4) * 4 + four)
    for k in range(1, n_space):
        greet(lax.rem(space + k, n_space), leaf)
    greet(space, other_y)
    greet(plane, other_y)
    greet(space, sibling)

    nodes_f[...] = jnp.zeros((3 * PLANE, 128), F32)
    for load in loads[:3]:
        load.wait()
    for c in range(3):
        base = c * PLANE
        value[0:64, 0:RANK] = leaf_nodes[c].astype(F32)
        value[64:72, 0:RANK] = one_nodes[c].astype(F32)
        for h in range(2):
            nodes_f[base : base + 36, h * RANK : (h + 1) * RANK] = value[pl.ds(h, 36, stride=2), 0:RANK]
        nodes_f[base + 36 : base + 37, 0:RANK] = two_nodes[c : c + 1].astype(F32)
    nodes[...] = nodes_f[...].astype(BF16)

    def remote(src, dst, send, came, s, l):
        return pltpu.make_async_remote_copy(
            src_ref=src, dst_ref=dst, send_sem=send, recv_sem=came, device_id=(s, l), device_id_type=MESH
        )

    mine = 4 + four
    parts = (None, pl.ds(0, CUT), pl.ds(CUT, 36 - CUT))

    def own(piece):
        return nodes if piece == 0 else coef.at[parts[piece]]

    def held(piece, slot):
        return node_tab.at[slot] if piece == 0 else coef_tab.at[slot, parts[piece]]

    def move(piece, src, slot, send, s, l):
        return remote(src, held(piece, slot), send, recv.at[piece, slot], s, l)

    def own_copies(piece):
        return (
            move(piece, own(piece), 4 + four, send_own.at[piece, 0], space, other_y),
            move(piece, own(piece), far + four, send_own.at[piece, 1], plane, other_y),
            move(piece, own(piece), mine, send_own.at[piece, 2], space, sibling),
        )

    def send_all(piece):
        for copy in own_copies(piece):
            copy.start()

    slot_a, slot_b, slot_c = 4 + four_y, near + four_y, near + four
    slot_z = (far + four_y, far + four)

    def arrived(piece, slot):
        move(piece, held(piece, slot), slot, send_own.at[piece, 0], space, sibling).wait_recv()

    def relay_copy(piece):
        return (
            move(piece, held(piece, slot_a), far + four_y, send_relay.at[piece], plane, other_y),
            move(piece, held(piece, slot_b), near + four_y, send_relay.at[piece], space, other_y),
        )

    def z_copy(piece, which):
        slot = (slot_b, slot_c)[which]
        return move(piece, held(piece, slot), slot_z[which], send_z.at[piece, which], ahead, leaf)

    def sib_copy(piece, which):
        slot = (slot_a, slot_b, slot_c) + slot_z
        return move(piece, held(piece, slot[which]), slot[which], send_sib.at[piece, which], space, sibling)

    def pass_ab(piece):
        by_a, by_b = relay_copy(piece)
        arrived(piece, slot_a)

        @pl.when(core == 0)
        def _():
            by_a.start()

        sib_copy(piece, 0).start()
        arrived(piece, slot_b)

        @pl.when(core == 1)
        def _():
            by_b.start()

        @pl.when(has_ahead)
        def _():
            z_copy(piece, 0).start()

        sib_copy(piece, 1).start()

    def pass_c(piece):
        arrived(piece, slot_c)

        @pl.when(has_ahead)
        def _():
            z_copy(piece, 1).start()

        sib_copy(piece, 2).start()

    def pass_z(piece):
        @pl.when(has_behind)
        def _():
            for which in range(2):
                arrived(piece, slot_z[which])
                sib_copy(piece, 3 + which).start()

    def leaves(i, carry):
        for j in range(4):
            pair = i * 4 + j
            halves = [
                nt(charges[:, pl.ds(pl.multiple_of((2 * pair + h) * 128, 128), 128)], basis[2 * pair + h])
                for h in range(2)
            ]
            coef[pair] = jnp.concatenate(halves, axis=1).astype(BF16)
        return carry

    pl.semaphore_wait(barrier, 3 + (n_space - 1) + 3)
    send_all(0)
    for k in range(1, 4):
        to = lax.rem(x + k, 4) * 4 + four
        remote(nodes, target_nodes.at[x], send_x.at[k], recv_x.at[x], space, to).start()
    loads[3].wait()
    loads[4].wait()
    lax.fori_loop(0, CUT // 4, leaves, 0)
    send_all(1)
    lax.fori_loop(CUT // 4, 8, leaves, 0)

    loads[5].wait()
    for i in range(4):
        halves = []
        for h in range(2):
            p = 2 * i + h
            stacked = jnp.concatenate([coef[4 * p + j] for j in range(4)], axis=1)
            halves.append(nt(stacked, t_one[p]))
        coef[32 + i] = jnp.concatenate(halves, axis=1).astype(BF16)
    send_all(2)
    pass_ab(0)

    loads[6].wait()
    top = nt(jnp.concatenate([coef[32 + j] for j in range(4)], axis=1), t_two[0])
    tx, ty, tz = (nodes_f[c * PLANE + 36 : c * PLANE + 37, 0:RANK] for c in range(3))
    rows = (tx, ty, tz) + split3(tx * tx + ty * ty + tz * tz)
    row = lax.broadcasted_iota(jnp.int32, (16, RANK), 0)
    feature = jnp.where((row >= 6) & (row < 9), 1.0, 0.0)
    for k, part in enumerate(rows):
        feature = jnp.where(row == k, jnp.broadcast_to(part, (16, RANK)), feature)
    entry[...] = jnp.concatenate([feature, top], axis=1).astype(BF16)

    own_two = four * n_space + space

    def two_copy(k):
        return remote(
            entry, two_tab.at[own_two], send_e.at[k], recv_e.at[space],
            lax.rem(space + k, n_space), leaf,
        )

    for k in range(1, n_space):
        two_copy(k).start()
    two_tab[own_two] = entry[...]

    for load in loads[7:]:
        load.wait()

    def code(links, per_dev, offset):
        owner = links // per_dev
        slot = (owner // 16 - space + 1) * 4 + owner % 4
        coded = owner // 4 % 4 * 1024 + slot * SLOT + offset + links % per_dev
        return jnp.where(links >= 0, coded, 4096)

    packed[0] = jnp.full((ROWS, 128), 4096, jnp.int32)
    packed[0, 0:64, 0:96] = code(leaf_links[...], LEAF_DEV, 0)
    packed[0, 64:72, 0:96] = code(one_links[...], ONE_DEV, LEAF_DEV)
    two = two_links[...]
    packed[0, 72:73, 0:96] = jnp.where(
        two >= 0, two // 4 % 4 * 1024 + TWO_AT + two % 4 * 16 + two // 16, 4096
    )
    codes = packed[0]
    group = codes // 1024
    before = jnp.where(
        lax.broadcasted_iota(jnp.int32, (128, 128), 0) < lax.broadcasted_iota(jnp.int32, (128, 128), 1), 1.0, 0.0
    ).astype(BF16)
    at = jnp.full((ROWS, 128), -1.0, F32)
    counts = []
    for q in range(4):
        member = jnp.where(group == q, 1.0, 0.0)
        rank = jnp.dot(member.astype(BF16), before, preferred_element_type=F32)
        at = jnp.where(group == q, rank + 128.0 * q, at)
        counts.append(jnp.sum(member, axis=1, keepdims=True))
    order[...] = at
    value[...] = (codes - group * 1024).astype(F32)
    lane = lax.broadcasted_iota(jnp.int32, (8, 128), 1)
    lane_f = lane.astype(F32)
    for q in range(4):
        packed[q] = jnp.broadcast_to(jnp.maximum((counts[q].astype(jnp.int32) + 3) // 4, 1), (ROWS, 128))
    pass_ab(1)

    def compact(b, carry):
        block = pl.ds(pl.multiple_of(b * 8, 8), 8)
        where = order[block, :]
        what = value[block, :]
        found = [jnp.full((8, 128), float(ZERO_AT), F32) for _ in range(4)]
        for j in range(96):
            w = jnp.broadcast_to(where[:, j : j + 1], (8, 128))
            v = jnp.broadcast_to(what[:, j : j + 1], (8, 128))
            for q in range(4):
                found[q] = jnp.where(w == lane_f + 128.0 * q, v, found[q])
        for q in range(4):
            packed[q, block, :] = jnp.where(lane == 127, packed[q, block, :], found[q].astype(jnp.int32))
        return carry

    lax.fori_loop(0, ROWS // 8, compact, 0)
    for k in range(1, 4):
        to = lax.rem(x + k, 4)
        remote(packed.at[to], lists.at[x], send_l.at[k], recv_l.at[x], space, to * 4 + four).start()
    keep_list = pltpu.make_async_copy(packed.at[x], lists.at[x], local_sem)
    keep_list.start()
    pass_c(0)
    pass_ab(2)
    pass_c(1)
    pass_z(0)

    def planes(source):
        px, py, pz = (source[c * PLANE : (c + 1) * PLANE, :].astype(F32) for c in range(3))
        return px, py, pz, split3(px * px + py * py + pz * pz)

    ones = jnp.ones((PLANE, 128), F32)
    zeros = jnp.zeros((PLANE, 128), F32)
    for k in range(6, 16):
        feat[pl.ds(k, PLANE, stride=16), :] = ones if k < 9 else zeros
    for k in range(3, 16):
        feat_t[pl.ds(k, PLANE, stride=16), :] = ones if k < 6 else zeros

    def table_copy(slot):
        part = pl.ds(slot * SLOT, SLOT)
        return pltpu.make_async_copy(table.at[part], table_out.at[part], out_sem.at[slot])

    def enter(slot, source, coefs):
        px, py, pz, norm = planes(source)
        for k, part in enumerate((px, py, pz) + norm):
            feat[pl.ds(k, PLANE, stride=16), :] = part

        def some(b, carry):
            for j in range(6):
                i = b * 6 + j
                f = feat[pl.ds(pl.multiple_of(i * 16, 16), 16), :].astype(BF16)
                c = coefs(i)
                table[slot * SLOT + 2 * i] = jnp.concatenate([f[:, :RANK], c[:, :RANK]], axis=1)
                table[slot * SLOT + 2 * i + 1] = jnp.concatenate([f[:, RANK:], c[:, RANK:]], axis=1)
            return carry

        lax.fori_loop(0, 6, some, 0)
        table_copy(slot).start()

    def enter_held(slot):
        enter(slot, node_tab.at[slot], lambda i: coef_tab[slot, i])

    def aim(which, source):
        px, py, pz, norm = planes(source)
        for k, part in enumerate((-2.0 * px, -2.0 * py, -2.0 * pz)):
            feat_t[pl.ds(k, PLANE, stride=16), :] = part
        for k, part in enumerate(norm):
            feat_t[pl.ds(6 + k, PLANE, stride=16), :] = part

        for b in range(BLOCKS):
            blocks[which * BLOCKS + b] = feat_t[b * 128 : (b + 1) * 128, :].T.astype(BF16)

    aim(x, nodes)
    pass_c(2)
    pass_z(1)
    enter(mine, nodes, lambda i: coef[i])
    table[pl.ds(ZERO_AT, 8)] = jnp.zeros((8, 16, 128), BF16)
    pass_z(2)

    for k in range(1, n_space):
        source = lax.rem(space + k, n_space)
        remote(
            entry, two_tab.at[four * n_space + source], send_e.at[0], recv_e.at[source], space, leaf
        ).wait_recv()

    def band(which):
        return two_tab.at[pl.ds(which * n_space, n_space)]

    def band_copy(k):
        which, to = ((four, other_y), (four, sibling), (four_y, sibling))[k]
        return remote(band(which), band(which), send_b.at[k], recv_b.at[which], space, to)

    def band_arrived(which):
        remote(band(which), band(which), send_b.at[0], recv_b.at[which], space, sibling).wait_recv()

    band_copy(0).start()
    band_copy(1).start()

    for k in range(1, 4):
        source = lax.rem(x + k, 4)
        remote(nodes, target_nodes.at[source], send_x.at[k], recv_x.at[source], space, leaf).wait_recv()
        aim(source, target_nodes.at[source])

    band_arrived(four_y)
    band_copy(2).start()

    for slot in (slot_a, slot_b, slot_c):
        enter_held(slot)

    def from_sibling(slot):
        for piece in range(PIECES):
            arrived(piece, slot)
        enter_held(slot)

    for slot in (4 + beside, 4 + beside_y, near + beside_y, near + beside):
        from_sibling(slot)

    @pl.when(has_behind)
    def _():
        for slot in slot_z:
            enter_held(slot)
        for slot in (far + beside_y, far + beside):
            from_sibling(slot)

    band_arrived(beside)
    band_arrived(beside_y)
    table[pl.ds(TWO_AT, 64)] = two_tab[...]
    rest = pl.ds(TWO_AT, ENTRIES - TWO_AT)
    ends = (
        pltpu.make_async_copy(table.at[rest], table_out.at[rest], out_sem.at[12]),
        pltpu.make_async_copy(blocks, blocks_out, out_sem.at[13]),
    )
    for copy in ends:
        copy.start()
    for k in range(1, 4):
        source = lax.rem(x + k, 4)
        remote(packed.at[0], lists.at[source], send_l.at[k], recv_l.at[source], space, leaf).wait_recv()

    for piece in range(PIECES):
        for copy in own_copies(piece):
            copy.wait_send()
        relay_copy(piece)[0].wait_send()
        for which in range(3):
            sib_copy(piece, which).wait_send()

        @pl.when(has_ahead)
        def _(piece=piece):
            for which in range(2):
                z_copy(piece, which).wait_send()

        @pl.when(has_behind)
        def _(piece=piece):
            for which in range(2):
                sib_copy(piece, 3 + which).wait_send()

    for k in range(1, n_space):
        two_copy(k).wait_send()
    for k in range(3):
        band_copy(k).wait_send()
    for k in range(1, 4):
        to = lax.rem(x + k, 4)
        remote(nodes, target_nodes.at[x], send_x.at[k], recv_x.at[x], space, to * 4 + four).wait_send()
        remote(packed.at[to], lists.at[x], send_l.at[k], recv_l.at[x], space, to * 4 + four).wait_send()
    keep_list.wait()
    for slot in (mine, slot_a, slot_b, slot_c, 4 + beside, 4 + beside_y, near + beside_y, near + beside):
        table_copy(slot).wait()

    @pl.when(has_behind)
    def _():
        for slot in slot_z + (far + beside_y, far + beside):
            table_copy(slot).wait()

    for copy in ends:
        copy.wait()


def upward(n_space, *arrays):
    hbm = pl.BlockSpec(memory_space=pltpu.HBM)
    dma = pltpu.SemaphoreType.DMA
    return pl.pallas_call(
        functools.partial(up_kernel, n_space),
        out_shape=(
            jax.ShapeDtypeStruct((ENTRIES, 16, 128), BF16),
            jax.ShapeDtypeStruct((4 * BLOCKS, 128, 128), BF16),
            jax.ShapeDtypeStruct((4, ROWS, 128), jnp.int32),
        ),
        in_specs=[hbm] * len(arrays),
        out_specs=[hbm] * 3,
        scratch_shapes=[pltpu.VMEM(a.shape, a.dtype) for a in arrays]
        + [
            pltpu.VMEM((3 * PLANE, 128), F32),
            pltpu.VMEM((3 * PLANE, 128), BF16),
            pltpu.VMEM((PAIRS, 16, 128), BF16),
            pltpu.VMEM((16, 128), BF16),
            pltpu.VMEM((4, ROWS, 128), jnp.int32),
            pltpu.VMEM((ROWS, 128), F32),
            pltpu.VMEM((ROWS, 128), F32),
            pltpu.VMEM((PLANE * 16, 128), F32),
            pltpu.VMEM((PLANE * 16, 128), F32),
            pltpu.VMEM((12, 3 * PLANE, 128), BF16),
            pltpu.VMEM((12, 36, 16, 128), BF16),
            pltpu.VMEM((64, 16, 128), BF16),
            pltpu.VMEM((4, 3 * PLANE, 128), BF16),
            pltpu.VMEM((ENTRIES, 16, 128), BF16),
            pltpu.VMEM((4 * BLOCKS, 128, 128), BF16),
            dma((len(arrays),)), dma((14,)),
            dma,
            dma((PIECES, 3)), dma((PIECES,)), dma((PIECES, 2)), dma((PIECES, 5)), dma((PIECES, 12)),
            dma((16,)), dma((16,)),
            dma((3,)), dma((4,)),
            dma((4,)), dma((4,)),
            dma((4,)), dma((4,)),
        ],
        compiler_params=pltpu.CompilerParams(
            collective_id=0, has_side_effects=True, vmem_limit_bytes=VMEM_BYTES
        ),
        name="upward",
    )(*arrays)


def couple_kernel(lists, table_in, blocks_in, out, table, blocks, targets, total, sem):
    loads = (
        pltpu.make_async_copy(blocks_in, blocks, sem.at[0]),
        pltpu.make_async_copy(table_in, table, sem.at[1]),
    )
    for load in loads:
        load.start()

    def clear(i, carry):
        for j in range(16):
            total[i * 16 + j] = jnp.zeros((16, RANK), F32)
        return carry

    lax.fori_loop(0, 4 * ROWS // 16, clear, 0)
    loads[0].wait()

    def spread(b, carry):
        block = blocks[b]
        for j in range(8):
            start = pl.multiple_of((b * 8 + j) * 128, 128)
            targets[pl.ds(start, 128), :] = block[:, 16 * j : 16 * j + 16]
        return carry

    lax.fori_loop(0, 4 * BLOCKS, spread, 0)
    loads[1].wait()

    end = 4 * ROWS - 1

    def step(carry):
        r, t, g = carry
        for _ in range(UNROLL):
            picked = [table[lists[r, 4 * g + i]] for i in range(4)]
            sources = jnp.concatenate([e[:, :RANK] for e in picked], axis=1)
            coefs = jnp.concatenate([e[:, RANK:] for e in picked], axis=1)
            mine = targets[pl.ds(pl.multiple_of(r * RANK, RANK), RANK), :]
            square = jnp.maximum(jnp.dot(mine, sources, preferred_element_type=F32), 1e-20)
            dist = square * lax.rsqrt(square)
            matrix = ((dist + 1.0 / SCALE) * jnp.exp2(dist * (-SCALE * LOG2E))).astype(BF16)
            total[r] += nt(coefs, matrix)
            done = g + 1 >= lists[r, 127]
            over = t == 72
            r = jnp.where(done, jnp.minimum(jnp.where(over, r + 8, r + 1), end), r)
            t = jnp.where(done, jnp.where(over, 0, t + 1), t)
            g = jnp.where(done, 0, g + 1)
        return r, t, g

    lax.while_loop(lambda c: c[0] < end, step, (jnp.int32(0), jnp.int32(0), jnp.int32(0)))

    def pack(i, carry):
        for q in range(4):
            at = q * ROWS + 2 * i
            both = jnp.concatenate([total[at], total[at + 1]], axis=1)
            out[q, i] = (both * (AMPLITUDE * SCALE)).astype(BF16)
        return carry

    lax.fori_loop(0, PAIRS, pack, 0)


def coupling(lists, table, blocks):
    hbm = pl.BlockSpec(memory_space=pltpu.HBM)
    return pl.pallas_call(
        couple_kernel,
        grid_spec=pltpu.PrefetchScalarGridSpec(
            num_scalar_prefetch=1,
            grid=(),
            in_specs=[hbm] * 2,
            out_specs=pl.BlockSpec(memory_space=pltpu.VMEM),
            scratch_shapes=[
                pltpu.VMEM((ENTRIES, 16, 128), BF16),
                pltpu.VMEM((4 * BLOCKS, 128, 128), BF16),
                pltpu.VMEM((4 * ROWS * RANK, 16), BF16),
                pltpu.VMEM((4 * ROWS, 16, RANK), F32),
                pltpu.SemaphoreType.DMA((2,)),
            ],
        ),
        out_shape=jax.ShapeDtypeStruct((4, PAIRS, 16, 128), BF16),
        compiler_params=pltpu.CompilerParams(vmem_limit_bytes=VMEM_BYTES),
        name="coupling",
    )(lists, table, blocks)


def down_kernel(
    far, basis_in, t_one_in, t_two_in, out, basis, t_one, t_two, came, near, in_sem, send, recv
):
    space = lax.axis_index("space")
    leaf = lax.axis_index("leaf")
    x = leaf // 4
    four = lax.rem(leaf, 4)
    loads = [
        pltpu.make_async_copy(src, dst, in_sem.at[k])
        for k, (src, dst) in enumerate(((t_two_in, t_two), (t_one_in, t_one), (basis_in, basis), (far.at[x], came.at[x])))
    ]
    for load in loads:
        load.start()
    barrier = pltpu.get_barrier_semaphore()
    for k in range(1, 4):
        to = lax.rem(x + k, 4) * 4 + four
        pl.semaphore_signal(barrier, inc=1, device_id=(space, to), device_id_type=MESH)
    pl.semaphore_wait(barrier, 3)

    def copy(k):
        to = lax.rem(x + k, 4)
        return pltpu.make_async_remote_copy(
            src_ref=far.at[to], dst_ref=came.at[x], send_sem=send.at[k], recv_sem=recv.at[x],
            device_id=(space, to * 4 + four), device_id_type=MESH,
        )

    for k in range(1, 4):
        copy(k).start()
    for load in loads:
        load.wait()
    for k in range(1, 4):
        source = lax.rem(x + k, 4)
        pltpu.make_async_remote_copy(
            src_ref=far.at[source], dst_ref=came.at[source], send_sem=send.at[k], recv_sem=recv.at[source],
            device_id=(space, leaf), device_id_type=MESH,
        ).wait_recv()

    def summed(i):
        return (
            came[0, i].astype(F32) + came[1, i].astype(F32)
            + came[2, i].astype(F32) + came[3, i].astype(F32)
        )

    local_two = summed(36)[:, :RANK].astype(BF16)
    down_one = jnp.dot(local_two, t_two[0], preferred_element_type=F32)
    for i in range(4):
        near[32 + i] = (summed(32 + i) + down_one[:, 128 * i : 128 * i + 128]).astype(BF16)

    def cluster(i, carry):
        both = near[32 + i]
        for h in range(2):
            local_one = both[:, h * RANK : (h + 1) * RANK]
            down_leaf = jnp.dot(local_one, t_one[2 * i + h], preferred_element_type=F32)
            for j in range(4):
                pair = 8 * i + 4 * h + j
                local_leaf = (summed(pair) + down_leaf[:, 128 * j : 128 * j + 128]).astype(BF16)
                for s in range(2):
                    at = pl.multiple_of((2 * pair + s) * 128, 128)
                    out[:, pl.ds(at, 128)] = jnp.dot(
                        local_leaf[:, s * RANK : (s + 1) * RANK], basis[2 * pair + s],
                        preferred_element_type=F32,
                    ).astype(BF16)
        return carry

    lax.fori_loop(0, 4, cluster, 0)
    for k in range(1, 4):
        copy(k).wait_send()


def downward(far, basis, t_one, t_two):
    hbm = pl.BlockSpec(memory_space=pltpu.HBM)
    dma = pltpu.SemaphoreType.DMA
    return pl.pallas_call(
        down_kernel,
        out_shape=jax.ShapeDtypeStruct((16, LEAF_DEV * 128), BF16),
        in_specs=[hbm] * 4,
        out_specs=pl.BlockSpec(memory_space=pltpu.VMEM),
        scratch_shapes=[pltpu.VMEM(a.shape, a.dtype) for a in (basis, t_one, t_two)]
        + [
            pltpu.VMEM((4, PAIRS, 16, 128), BF16),
            pltpu.VMEM((36, 16, 128), BF16),
            dma((4,)), dma((4,)), dma((4,)),
        ],
        compiler_params=pltpu.CompilerParams(
            collective_id=1, has_side_effects=True, vmem_limit_bytes=VMEM_BYTES
        ),
        name="downward",
    )(far, basis, t_one, t_two)


def local(
    charges, leaf_basis, transfer_one, transfer_two, nodes_leaf, nodes_one, nodes_two,
    links_leaf, links_one, links_two,
):
    table, blocks, lists = upward(
        lax.axis_size("space"), charges, leaf_basis, transfer_one, transfer_two,
        nodes_leaf.transpose(1, 0, 2), nodes_one.transpose(1, 0, 2), nodes_two.reshape(3, RANK),
        links_leaf, links_one, links_two,
    )
    far = coupling(lists.reshape(4 * ROWS, 128), table, blocks)
    return downward(far, leaf_basis, transfer_one, transfer_two)


def solution(mesh):
    return jax.shard_map(
        local,
        mesh=mesh,
        in_specs=(
            P(None, ("space", "leaf")),
            P(("space", "leaf"), None, None),
            P(("space", "leaf"), None, None),
            P(("space", "leaf"), None, None),
            P(("space", "leaf"), None, None),
            P(("space", "leaf"), None, None),
            P(("space", "leaf"), None, None),
            P(("space", "leaf"), None),
            P(("space", "leaf"), None),
            P(("space", "leaf"), None),
        ),
        out_specs=P(None, ("space", "leaf")),
        check_vma=False,
    )
```

```python
import functools

import jax
import jax.numpy as jnp
from jax import lax
from jax.experimental import pallas as pl
from jax.experimental.pallas import tpu as pltpu
from jax.sharding import PartitionSpec as P

SCALE = 1.7320508075688772 / 2.0
AMPLITUDE = 0.25
LOG2E = 1.4426950408889634
MESH = pl.DeviceIdType.MESH
F32 = jnp.float32
BF16 = jnp.bfloat16

RANK = 64
LEAF_DEV = 64
ONE_DEV = 8
PAIRS = 37
PLANE = 48
ROWS = 80
SLOT = 72
TWO_AT = 12 * SLOT
ZERO_AT = TWO_AT + 64
ENTRIES = ZERO_AT + 8
UNROLL = 96

PIECES = 3
CUT = 16
BLOCKS = 5
VMEM_BYTES = 58 * 1024 * 1024
DOWN_BYTES = 53 * 1024 * 1024 + 512 * 1024


def nt(a, b):
    return lax.dot_general(a, b, (((1,), (1,)), ((), ())), preferred_element_type=F32)


def split3(value):
    first = value.astype(BF16).astype(F32)
    rest = value - first
    second = rest.astype(BF16).astype(F32)
    return first, second, rest - second


def up_kernel(
    n_space,
    charges_in, basis_in, t_one_in, t_two_in, leaf_nodes_in, one_nodes_in, two_nodes_in,
    leaf_links_in, one_links_in, two_links_in,
    table_out, blocks_out, lists,
    charges, basis, t_one, t_two, leaf_nodes, one_nodes, two_nodes, leaf_links, one_links, two_links,
    nodes_f, nodes, coef, entry, packed, order, value, feat, feat_t,
    node_tab, coef_tab, two_tab, target_nodes, table, blocks,
    in_sem, out_sem, local_sem, send_own, send_relay, send_z, send_sib, recv,
    send_e, recv_e, send_b, recv_b, send_x, recv_x, send_l, recv_l,
):
    space = lax.axis_index("space")
    leaf = lax.axis_index("leaf")
    x = leaf // 4
    four = lax.rem(leaf, 4)
    y_lo = four // 2
    core = lax.rem(four, 2)
    four_y = (1 - y_lo) * 2 + core
    beside = y_lo * 2 + (1 - core)
    beside_y = (1 - y_lo) * 2 + (1 - core)
    other_y = x * 4 + four_y
    sibling = x * 4 + beside
    side = 1 - 2 * lax.rem(space, 2)
    plane = space + side
    ahead = space + 2 * side
    behind = space - 2 * side
    has_ahead = (ahead >= 0) & (ahead < n_space)
    has_behind = (behind >= 0) & (behind < n_space)
    near, far = (1 + side) * 4, (1 - side) * 4

    loads = [
        pltpu.make_async_copy(src, dst, in_sem.at[k])
        for k, (src, dst) in enumerate(
            (
                (leaf_nodes_in, leaf_nodes), (one_nodes_in, one_nodes), (two_nodes_in, two_nodes),
                (charges_in, charges), (basis_in, basis), (t_one_in, t_one), (t_two_in, t_two),
                (leaf_links_in, leaf_links), (one_links_in, one_links), (two_links_in, two_links),
            )
        )
    ]
    for load in loads:
        load.start()

    barrier = pltpu.get_barrier_semaphore()

    def greet(s, l):
        pl.semaphore_signal(barrier, inc=1, device_id=(s, l), device_id_type=MESH)

    for k in range(1, 4):
        greet(space, lax.rem(x + k, 4) * 4 + four)
    for k in range(1, n_space):
        greet(lax.rem(space + k, n_space), leaf)
    greet(space, other_y)
    greet(plane, other_y)
    greet(space, sibling)

    nodes_f[...] = jnp.zeros((3 * PLANE, 128), F32)
    for load in loads[:3]:
        load.wait()
    for c in range(3):
        base = c * PLANE
        value[0:64, 0:RANK] = leaf_nodes[c].astype(F32)
        value[64:72, 0:RANK] = one_nodes[c].astype(F32)
        for h in range(2):
            nodes_f[base : base + 36, h * RANK : (h + 1) * RANK] = value[pl.ds(h, 36, stride=2), 0:RANK]
        nodes_f[base + 36 : base + 37, 0:RANK] = two_nodes[c : c + 1].astype(F32)
    nodes[...] = nodes_f[...].astype(BF16)

    def remote(src, dst, send, came, s, l):
        return pltpu.make_async_remote_copy(
            src_ref=src, dst_ref=dst, send_sem=send, recv_sem=came, device_id=(s, l), device_id_type=MESH
        )

    mine = 4 + four
    parts = (None, pl.ds(0, CUT), pl.ds(CUT, 36 - CUT))

    def own(piece):
        return nodes if piece == 0 else coef.at[parts[piece]]

    def held(piece, slot):
        return node_tab.at[slot] if piece == 0 else coef_tab.at[slot, parts[piece]]

    def move(piece, src, slot, send, s, l):
        return remote(src, held(piece, slot), send, recv.at[piece, slot], s, l)

    def own_copies(piece):
        return (
            move(piece, own(piece), 4 + four, send_own.at[piece, 0], space, other_y),
            move(piece, own(piece), far + four, send_own.at[piece, 1], plane, other_y),
            move(piece, own(piece), mine, send_own.at[piece, 2], space, sibling),
        )

    def send_all(piece):
        for copy in own_copies(piece):
            copy.start()

    slot_a, slot_b, slot_c = 4 + four_y, near + four_y, near + four
    slot_z = (far + four_y, far + four)

    def arrived(piece, slot):
        move(piece, held(piece, slot), slot, send_own.at[piece, 0], space, sibling).wait_recv()

    def relay_copy(piece):
        return (
            move(piece, held(piece, slot_a), far + four_y, send_relay.at[piece], plane, other_y),
            move(piece, held(piece, slot_b), near + four_y, send_relay.at[piece], space, other_y),
        )

    def z_copy(piece, which):
        slot = (slot_b, slot_c)[which]
        return move(piece, held(piece, slot), slot_z[which], send_z.at[piece, which], ahead, leaf)

    def sib_copy(piece, which):
        slot = (slot_a, slot_b, slot_c) + slot_z
        return move(piece, held(piece, slot[which]), slot[which], send_sib.at[piece, which], space, sibling)

    def pass_ab(piece):
        by_a, by_b = relay_copy(piece)
        arrived(piece, slot_a)

        @pl.when(core == 0)
        def _():
            by_a.start()

        sib_copy(piece, 0).start()
        arrived(piece, slot_b)

        @pl.when(core == 1)
        def _():
            by_b.start()

        @pl.when(has_ahead)
        def _():
            z_copy(piece, 0).start()

        sib_copy(piece, 1).start()

    def pass_c(piece):
        arrived(piece, slot_c)

        @pl.when(has_ahead)
        def _():
            z_copy(piece, 1).start()

        sib_copy(piece, 2).start()

    def pass_z(piece):
        @pl.when(has_behind)
        def _():
            for which in range(2):
                arrived(piece, slot_z[which])
                sib_copy(piece, 3 + which).start()

    def leaves(i, carry):
        for j in range(4):
            pair = i * 4 + j
            halves = [
                nt(charges[:, pl.ds(pl.multiple_of((2 * pair + h) * 128, 128), 128)], basis[2 * pair + h])
                for h in range(2)
            ]
            coef[pair] = jnp.concatenate(halves, axis=1).astype(BF16)
        return carry

    pl.semaphore_wait(barrier, 3 + (n_space - 1) + 3)
    send_all(0)
    for k in range(1, 4):
        to = lax.rem(x + k, 4) * 4 + four
        remote(nodes, target_nodes.at[x], send_x.at[k], recv_x.at[x], space, to).start()
    loads[3].wait()
    loads[4].wait()
    lax.fori_loop(0, CUT // 4, leaves, 0)
    send_all(1)
    lax.fori_loop(CUT // 4, 8, leaves, 0)

    loads[5].wait()
    for i in range(4):
        halves = []
        for h in range(2):
            p = 2 * i + h
            stacked = jnp.concatenate([coef[4 * p + j] for j in range(4)], axis=1)
            halves.append(nt(stacked, t_one[p]))
        coef[32 + i] = jnp.concatenate(halves, axis=1).astype(BF16)
    loads[6].wait()
    top = nt(jnp.concatenate([coef[32 + j] for j in range(4)], axis=1), t_two[0])
    tx, ty, tz = (nodes_f[c * PLANE + 36 : c * PLANE + 37, 0:RANK] for c in range(3))
    rows = (tx, ty, tz) + split3(tx * tx + ty * ty + tz * tz)
    row = lax.broadcasted_iota(jnp.int32, (16, RANK), 0)
    feature = jnp.where((row >= 6) & (row < 9), 1.0, 0.0)
    for k, part in enumerate(rows):
        feature = jnp.where(row == k, jnp.broadcast_to(part, (16, RANK)), feature)
    entry[...] = jnp.concatenate([feature, top], axis=1).astype(BF16)

    own_two = four * n_space + space

    def two_copy(k):
        return remote(
            entry, two_tab.at[own_two], send_e.at[k], recv_e.at[space],
            lax.rem(space + k, n_space), leaf,
        )

    for k in range(1, n_space):
        two_copy(k).start()
    send_all(2)
    two_tab[own_two] = entry[...]
    pass_ab(0)
    pass_ab(1)

    for load in loads[7:]:
        load.wait()

    def code(links, per_dev, offset):
        owner = links // per_dev
        slot = (owner // 16 - space + 1) * 4 + owner % 4
        coded = owner // 4 % 4 * 1024 + slot * SLOT + offset + links % per_dev
        return jnp.where(links >= 0, coded, 4096)

    packed[0] = jnp.full((ROWS, 128), 4096, jnp.int32)
    packed[0, 0:64, 0:96] = code(leaf_links[...], LEAF_DEV, 0)
    packed[0, 64:72, 0:96] = code(one_links[...], ONE_DEV, LEAF_DEV)
    two = two_links[...]
    packed[0, 72:73, 0:96] = jnp.where(
        two >= 0, two // 4 % 4 * 1024 + TWO_AT + two % 4 * 16 + two // 16, 4096
    )
    codes = packed[0]
    group = codes // 1024
    before = jnp.where(
        lax.broadcasted_iota(jnp.int32, (128, 128), 0) < lax.broadcasted_iota(jnp.int32, (128, 128), 1), 1.0, 0.0
    ).astype(BF16)
    at = jnp.full((ROWS, 128), -1.0, F32)
    counts = []
    for q in range(4):
        member = jnp.where(group == q, 1.0, 0.0)
        rank = jnp.dot(member.astype(BF16), before, preferred_element_type=F32)
        at = jnp.where(group == q, rank + 128.0 * q, at)
        counts.append(jnp.sum(member, axis=1, keepdims=True))
    order[...] = at
    value[...] = (codes - group * 1024).astype(F32)
    lane = lax.broadcasted_iota(jnp.int32, (8, 128), 1)
    lane_f = lane.astype(F32)
    for q in range(4):
        packed[q] = jnp.broadcast_to(jnp.maximum((counts[q].astype(jnp.int32) + 3) // 4, 1), (ROWS, 128))

    def compact(b, carry):
        block = pl.ds(pl.multiple_of(b * 8, 8), 8)
        where = order[block, :]
        what = value[block, :]
        found = [jnp.full((8, 128), float(ZERO_AT), F32) for _ in range(4)]
        for j in range(96):
            w = jnp.broadcast_to(where[:, j : j + 1], (8, 128))
            v = jnp.broadcast_to(what[:, j : j + 1], (8, 128))
            for q in range(4):
                found[q] = jnp.where(w == lane_f + 128.0 * q, v, found[q])
        for q in range(4):
            packed[q, block, :] = jnp.where(lane == 127, packed[q, block, :], found[q].astype(jnp.int32))
        return carry

    lax.fori_loop(0, 4, compact, 0)
    pass_ab(2)
    lax.fori_loop(4, ROWS // 8, compact, 0)
    for k in range(1, 4):
        to = lax.rem(x + k, 4)
        remote(packed.at[to], lists.at[x], send_l.at[k], recv_l.at[x], space, to * 4 + four).start()
    keep_list = pltpu.make_async_copy(packed.at[x], lists.at[x], local_sem)
    keep_list.start()
    pass_c(0)
    pass_c(1)

    def planes(source):
        px, py, pz = (source[c * PLANE : (c + 1) * PLANE, :].astype(F32) for c in range(3))
        return px, py, pz, split3(px * px + py * py + pz * pz)

    ones = jnp.ones((PLANE, 128), F32)
    zeros = jnp.zeros((PLANE, 128), F32)
    for k in range(6, 16):
        feat[pl.ds(k, PLANE, stride=16), :] = ones if k < 9 else zeros
    for k in range(3, 16):
        feat_t[pl.ds(k, PLANE, stride=16), :] = ones if k < 6 else zeros

    def table_copy(slot):
        part = pl.ds(slot * SLOT, SLOT)
        return pltpu.make_async_copy(table.at[part], table_out.at[part], out_sem.at[slot])

    def enter(slot, source, coefs):
        px, py, pz, norm = planes(source)
        for k, part in enumerate((px, py, pz) + norm):
            feat[pl.ds(k, PLANE, stride=16), :] = part

        def some(b, carry):
            for j in range(12):
                i = b * 12 + j
                f = feat[pl.ds(pl.multiple_of(i * 16, 16), 16), :].astype(BF16)
                c = coefs(i)
                table[slot * SLOT + 2 * i] = jnp.concatenate([f[:, :RANK], c[:, :RANK]], axis=1)
                table[slot * SLOT + 2 * i + 1] = jnp.concatenate([f[:, RANK:], c[:, RANK:]], axis=1)
            return carry

        lax.fori_loop(0, 3, some, 0)
        table_copy(slot).start()

    def enter_held(slot):
        enter(slot, node_tab.at[slot], lambda i: coef_tab[slot, i])

    def aim(which, source):
        px, py, pz, norm = planes(source)
        for k, part in enumerate((-2.0 * px, -2.0 * py, -2.0 * pz)):
            feat_t[pl.ds(k, PLANE, stride=16), :] = part
        for k, part in enumerate(norm):
            feat_t[pl.ds(6 + k, PLANE, stride=16), :] = part

        for b in range(BLOCKS):
            blocks[which * BLOCKS + b] = feat_t[b * 128 : (b + 1) * 128, :].T.astype(BF16)

    enter(mine, nodes, lambda i: coef[i])
    table[pl.ds(ZERO_AT, 8)] = jnp.zeros((8, 16, 128), BF16)
    pass_c(2)
    pass_z(0)
    pass_z(1)

    for k in range(1, n_space):
        source = lax.rem(space + k, n_space)
        remote(
            entry, two_tab.at[four * n_space + source], send_e.at[0], recv_e.at[source], space, leaf
        ).wait_recv()

    def band(which):
        return two_tab.at[pl.ds(which * n_space, n_space)]

    def band_copy(k):
        which, to = ((four, other_y), (four, sibling), (four_y, sibling))[k]
        return remote(band(which), band(which), send_b.at[k], recv_b.at[which], space, to)

    def band_arrived(which):
        remote(band(which), band(which), send_b.at[0], recv_b.at[which], space, sibling).wait_recv()

    band_copy(0).start()
    band_copy(1).start()
    for slot in (slot_a, slot_b):
        enter_held(slot)
    pass_z(2)
    band_arrived(four_y)
    band_copy(2).start()
    aim(x, nodes)
    for k in range(1, 4):
        source = lax.rem(x + k, 4)
        remote(nodes, target_nodes.at[source], send_x.at[k], recv_x.at[source], space, leaf).wait_recv()
        aim(source, target_nodes.at[source])
    blocks_copy = pltpu.make_async_copy(blocks, blocks_out, out_sem.at[13])
    blocks_copy.start()
    enter_held(slot_c)

    def from_sibling(slot):
        for piece in range(PIECES):
            arrived(piece, slot)
        enter_held(slot)

    for slot in (4 + beside, 4 + beside_y, near + beside_y, near + beside):
        from_sibling(slot)

    @pl.when(has_behind)
    def _():
        for slot in slot_z:
            enter_held(slot)
        for slot in (far + beside_y, far + beside):
            from_sibling(slot)

    band_arrived(beside)
    band_arrived(beside_y)
    table[pl.ds(TWO_AT, 64)] = two_tab[...]
    rest = pl.ds(TWO_AT, ENTRIES - TWO_AT)
    rest_copy = pltpu.make_async_copy(table.at[rest], table_out.at[rest], out_sem.at[12])
    rest_copy.start()
    for k in range(1, 4):
        source = lax.rem(x + k, 4)
        remote(packed.at[0], lists.at[source], send_l.at[k], recv_l.at[source], space, leaf).wait_recv()

    for piece in range(PIECES):
        for copy in own_copies(piece):
            copy.wait_send()
        relay_copy(piece)[0].wait_send()
        for which in range(3):
            sib_copy(piece, which).wait_send()

        @pl.when(has_ahead)
        def _(piece=piece):
            for which in range(2):
                z_copy(piece, which).wait_send()

        @pl.when(has_behind)
        def _(piece=piece):
            for which in range(2):
                sib_copy(piece, 3 + which).wait_send()

    for k in range(1, n_space):
        two_copy(k).wait_send()
    for k in range(3):
        band_copy(k).wait_send()
    for k in range(1, 4):
        to = lax.rem(x + k, 4)
        remote(nodes, target_nodes.at[x], send_x.at[k], recv_x.at[x], space, to * 4 + four).wait_send()
        remote(packed.at[to], lists.at[x], send_l.at[k], recv_l.at[x], space, to * 4 + four).wait_send()
    keep_list.wait()
    for slot in (mine, slot_a, slot_b, slot_c, 4 + beside, 4 + beside_y, near + beside_y, near + beside):
        table_copy(slot).wait()

    @pl.when(has_behind)
    def _():
        for slot in slot_z + (far + beside_y, far + beside):
            table_copy(slot).wait()

    rest_copy.wait()
    blocks_copy.wait()


def upward(n_space, *arrays):
    hbm = pl.BlockSpec(memory_space=pltpu.HBM)
    dma = pltpu.SemaphoreType.DMA
    return pl.pallas_call(
        functools.partial(up_kernel, n_space),
        out_shape=(
            jax.ShapeDtypeStruct((ENTRIES, 16, 128), BF16),
            jax.ShapeDtypeStruct((4 * BLOCKS, 128, 128), BF16),
            jax.ShapeDtypeStruct((4, ROWS, 128), jnp.int32),
        ),
        in_specs=[hbm] * len(arrays),
        out_specs=[hbm] * 3,
        scratch_shapes=[pltpu.VMEM(a.shape, a.dtype) for a in arrays]
        + [
            pltpu.VMEM((3 * PLANE, 128), F32),
            pltpu.VMEM((3 * PLANE, 128), BF16),
            pltpu.VMEM((PAIRS, 16, 128), BF16),
            pltpu.VMEM((16, 128), BF16),
            pltpu.VMEM((4, ROWS, 128), jnp.int32),
            pltpu.VMEM((ROWS, 128), F32),
            pltpu.VMEM((ROWS, 128), F32),
            pltpu.VMEM((PLANE * 16, 128), F32),
            pltpu.VMEM((PLANE * 16, 128), F32),
            pltpu.VMEM((12, 3 * PLANE, 128), BF16),
            pltpu.VMEM((12, 36, 16, 128), BF16),
            pltpu.VMEM((64, 16, 128), BF16),
            pltpu.VMEM((4, 3 * PLANE, 128), BF16),
            pltpu.VMEM((ENTRIES, 16, 128), BF16),
            pltpu.VMEM((4 * BLOCKS, 128, 128), BF16),
            dma((len(arrays),)), dma((14,)),
            dma,
            dma((PIECES, 3)), dma((PIECES,)), dma((PIECES, 2)), dma((PIECES, 5)), dma((PIECES, 12)),
            dma((16,)), dma((16,)),
            dma((3,)), dma((4,)),
            dma((4,)), dma((4,)),
            dma((4,)), dma((4,)),
        ],
        compiler_params=pltpu.CompilerParams(
            collective_id=0, has_side_effects=True, vmem_limit_bytes=VMEM_BYTES
        ),
        name="upward",
    )(*arrays)


def couple_kernel(lists, table_in, blocks_in, out, table, blocks, targets, total, sem):
    loads = (
        pltpu.make_async_copy(blocks_in, blocks, sem.at[0]),
        pltpu.make_async_copy(table_in, table, sem.at[1]),
    )
    for load in loads:
        load.start()

    def clear(i, carry):
        for j in range(16):
            total[i * 16 + j] = jnp.zeros((16, RANK), F32)
        return carry

    lax.fori_loop(0, 4 * ROWS // 16, clear, 0)
    loads[0].wait()

    def spread(q, carry):
        for i in range(BLOCKS):
            block = blocks[q * BLOCKS + i]
            for j in range(8):
                start = pl.multiple_of(((q * BLOCKS + i) * 8 + j) * 128, 128)
                targets[pl.ds(start, 128), :] = block[:, 16 * j : 16 * j + 16]
        return carry

    lax.fori_loop(0, 4, spread, 0)
    loads[1].wait()

    end = 4 * ROWS - 1

    def step(carry):
        r, t, g = carry
        for _ in range(UNROLL):
            picked = [table[lists[r, 4 * g + i]] for i in range(4)]
            sources = jnp.concatenate([e[:, :RANK] for e in picked], axis=1)
            coefs = jnp.concatenate([e[:, RANK:] for e in picked], axis=1)
            mine = targets[pl.ds(pl.multiple_of(r * RANK, RANK), RANK), :]
            square = jnp.maximum(jnp.dot(mine, sources, preferred_element_type=F32), 1e-20)
            dist = square * lax.rsqrt(square)
            matrix = ((dist + 1.0 / SCALE) * jnp.exp2(dist * (-SCALE * LOG2E))).astype(BF16)
            total[r] += nt(coefs, matrix)
            done = g + 1 >= lists[r, 127]
            over = t == 72
            r = jnp.where(done, jnp.minimum(jnp.where(over, r + 8, r + 1), end), r)
            t = jnp.where(done, jnp.where(over, 0, t + 1), t)
            g = jnp.where(done, 0, g + 1)
        return r, t, g

    lax.while_loop(lambda c: c[0] < end, step, (jnp.int32(0), jnp.int32(0), jnp.int32(0)))

    def pack(q, carry):
        for i in range(PAIRS):
            at = q * ROWS + 2 * i
            both = jnp.concatenate([total[at], total[at + 1]], axis=1)
            out[q, i] = (both * (AMPLITUDE * SCALE)).astype(BF16)
        return carry

    lax.fori_loop(0, 4, pack, 0)


def coupling(lists, table, blocks):
    hbm = pl.BlockSpec(memory_space=pltpu.HBM)
    return pl.pallas_call(
        couple_kernel,
        grid_spec=pltpu.PrefetchScalarGridSpec(
            num_scalar_prefetch=1,
            grid=(),
            in_specs=[hbm] * 2,
            out_specs=pl.BlockSpec(memory_space=pltpu.VMEM),
            scratch_shapes=[
                pltpu.VMEM((ENTRIES, 16, 128), BF16),
                pltpu.VMEM((4 * BLOCKS, 128, 128), BF16),
                pltpu.VMEM((4 * ROWS * RANK, 16), BF16),
                pltpu.VMEM((4 * ROWS, 16, RANK), F32),
                pltpu.SemaphoreType.DMA((2,)),
            ],
        ),
        out_shape=jax.ShapeDtypeStruct((4, PAIRS, 16, 128), BF16),
        compiler_params=pltpu.CompilerParams(vmem_limit_bytes=VMEM_BYTES),
        name="coupling",
    )(lists, table, blocks)


def down_kernel(
    far, basis_in, t_one_in, t_two_in, out, basis, t_one, t_two, came, near, in_sem, send, recv
):
    space = lax.axis_index("space")
    leaf = lax.axis_index("leaf")
    x = leaf // 4
    four = lax.rem(leaf, 4)
    loads = [
        pltpu.make_async_copy(src, dst, in_sem.at[k])
        for k, (src, dst) in enumerate(((t_two_in, t_two), (t_one_in, t_one), (basis_in, basis), (far.at[x], came.at[x])))
    ]
    for load in loads:
        load.start()
    barrier = pltpu.get_barrier_semaphore()
    for k in range(1, 4):
        to = lax.rem(x + k, 4) * 4 + four
        pl.semaphore_signal(barrier, inc=1, device_id=(space, to), device_id_type=MESH)
    pl.semaphore_wait(barrier, 3)

    def copy(k):
        to = lax.rem(x + k, 4)
        return pltpu.make_async_remote_copy(
            src_ref=far.at[to], dst_ref=came.at[x], send_sem=send.at[k], recv_sem=recv.at[x],
            device_id=(space, to * 4 + four), device_id_type=MESH,
        )

    for k in range(1, 4):
        copy(k).start()
    for load in loads:
        load.wait()
    for k in range(1, 4):
        source = lax.rem(x + k, 4)
        pltpu.make_async_remote_copy(
            src_ref=far.at[source], dst_ref=came.at[source], send_sem=send.at[k], recv_sem=recv.at[source],
            device_id=(space, leaf), device_id_type=MESH,
        ).wait_recv()

    def summed(i):
        return (
            came[0, i].astype(F32) + came[1, i].astype(F32)
            + came[2, i].astype(F32) + came[3, i].astype(F32)
        )

    local_two = summed(36)[:, :RANK].astype(BF16)
    down_one = jnp.dot(local_two, t_two[0], preferred_element_type=F32)
    for i in range(4):
        near[32 + i] = (summed(32 + i) + down_one[:, 128 * i : 128 * i + 128]).astype(BF16)

    def cluster(i, carry):
        both = near[32 + i]
        for h in range(2):
            local_one = both[:, h * RANK : (h + 1) * RANK]
            down_leaf = jnp.dot(local_one, t_one[2 * i + h], preferred_element_type=F32)
            for j in range(4):
                pair = 8 * i + 4 * h + j
                local_leaf = (summed(pair) + down_leaf[:, 128 * j : 128 * j + 128]).astype(BF16)
                for s in range(2):
                    at = pl.multiple_of((2 * pair + s) * 128, 128)
                    out[:, pl.ds(at, 128)] = jnp.dot(
                        local_leaf[:, s * RANK : (s + 1) * RANK], basis[2 * pair + s],
                        preferred_element_type=F32,
                    ).astype(BF16)
        return carry

    lax.fori_loop(0, 4, cluster, 0)
    for k in range(1, 4):
        copy(k).wait_send()


def downward(far, basis, t_one, t_two):
    hbm = pl.BlockSpec(memory_space=pltpu.HBM)
    dma = pltpu.SemaphoreType.DMA
    return pl.pallas_call(
        down_kernel,
        out_shape=jax.ShapeDtypeStruct((16, LEAF_DEV * 128), BF16),
        in_specs=[hbm] * 4,
        out_specs=pl.BlockSpec(memory_space=pltpu.VMEM),
        scratch_shapes=[pltpu.VMEM(a.shape, a.dtype) for a in (basis, t_one, t_two)]
        + [
            pltpu.VMEM((4, PAIRS, 16, 128), BF16),
            pltpu.VMEM((36, 16, 128), BF16),
            dma((4,)), dma((4,)), dma((4,)),
        ],
        compiler_params=pltpu.CompilerParams(
            collective_id=1, has_side_effects=True, vmem_limit_bytes=DOWN_BYTES
        ),
        name="downward",
    )(far, basis, t_one, t_two)


def local(
    charges, leaf_basis, transfer_one, transfer_two, nodes_leaf, nodes_one, nodes_two,
    links_leaf, links_one, links_two,
):
    table, blocks, lists = upward(
        lax.axis_size("space"), charges, leaf_basis, transfer_one, transfer_two,
        nodes_leaf.transpose(1, 0, 2), nodes_one.transpose(1, 0, 2), nodes_two.reshape(3, RANK),
        links_leaf, links_one, links_two,
    )
    far = coupling(lists.reshape(4 * ROWS, 128), table, blocks)
    return downward(far, leaf_basis, transfer_one, transfer_two)


def solution(mesh):
    return jax.shard_map(
        local,
        mesh=mesh,
        in_specs=(
            P(None, ("space", "leaf")),
            P(("space", "leaf"), None, None),
            P(("space", "leaf"), None, None),
            P(("space", "leaf"), None, None),
            P(("space", "leaf"), None, None),
            P(("space", "leaf"), None, None),
            P(("space", "leaf"), None, None),
            P(("space", "leaf"), None),
            P(("space", "leaf"), None),
            P(("space", "leaf"), None),
        ),
        out_specs=P(None, ("space", "leaf")),
        check_vma=False,
    )
```

```python
import functools

import jax
import jax.numpy as jnp
from jax import lax
from jax.experimental import pallas as pl
from jax.experimental.pallas import tpu as pltpu
from jax.sharding import PartitionSpec as P

SCALE = 1.7320508075688772 / 2.0
AMPLITUDE = 0.25
LOG2E = 1.4426950408889634
MESH = pl.DeviceIdType.MESH
F32 = jnp.float32
BF16 = jnp.bfloat16

RANK = 64
LEAF_DEV = 64
ONE_DEV = 8
PAIRS = 37
PLANE = 48
CLASS_ROWS = 24
CLASS_PAIRS = 10
ROWS = 4 * CLASS_ROWS
HOMES = 16
ALL_ROWS = HOMES * CLASS_ROWS
SLOT = 72
TWO_AT = 12 * SLOT
ZERO_AT = TWO_AT + 64
ENTRIES = ZERO_AT + 8
UNROLL = 96

PIECES = 3
CUT = 16
BLOCKS = 2
VMEM_BYTES = 58 * 1024 * 1024
DOWN_BYTES = 53 * 1024 * 1024 + 512 * 1024


def nt(a, b):
    return lax.dot_general(a, b, (((1,), (1,)), ((), ())), preferred_element_type=F32)


def other_four(y_lo, core, kind):
    return (1 - y_lo if kind >= 2 else y_lo) * 2 + (1 - core if kind % 2 else core)


def block_peers():
    return [(k, kind) for k in range(4) for kind in range(4) if (k, kind) != (0, 0)]


def split3(value):
    first = value.astype(BF16).astype(F32)
    rest = value - first
    second = rest.astype(BF16).astype(F32)
    return first, second, rest - second


def up_kernel(
    n_space,
    charges_in, basis_in, t_one_in, t_two_in, leaf_nodes_in, one_nodes_in, two_nodes_in,
    leaf_links_in, one_links_in, two_links_in,
    table_out, blocks_out, lists,
    charges, basis, t_one, t_two, leaf_nodes, one_nodes, two_nodes, leaf_links, one_links, two_links,
    nodes_f, nodes, nodes_t, coef, entry, packed, order, value, feat, feat_t,
    node_tab, coef_tab, two_tab, target_nodes, table, blocks,
    in_sem, out_sem, local_sem, send_own, send_relay, send_z, send_sib, recv,
    send_e, recv_e, send_b, recv_b, send_x, recv_x, send_l, recv_l,
):
    space = lax.axis_index("space")
    leaf = lax.axis_index("leaf")
    x = leaf // 4
    four = lax.rem(leaf, 4)
    y_lo = four // 2
    core = lax.rem(four, 2)
    four_y = (1 - y_lo) * 2 + core
    beside = y_lo * 2 + (1 - core)
    beside_y = (1 - y_lo) * 2 + (1 - core)
    other_y = x * 4 + four_y
    sibling = x * 4 + beside
    side = 1 - 2 * lax.rem(space, 2)
    plane = space + side
    ahead = space + 2 * side
    behind = space - 2 * side
    has_ahead = (ahead >= 0) & (ahead < n_space)
    has_behind = (behind >= 0) & (behind < n_space)
    near, far = (1 + side) * 4, (1 - side) * 4

    loads = [
        pltpu.make_async_copy(src, dst, in_sem.at[k])
        for k, (src, dst) in enumerate(
            (
                (leaf_nodes_in, leaf_nodes), (one_nodes_in, one_nodes), (two_nodes_in, two_nodes),
                (charges_in, charges), (basis_in, basis), (t_one_in, t_one), (t_two_in, t_two),
                (leaf_links_in, leaf_links), (one_links_in, one_links), (two_links_in, two_links),
            )
        )
    ]
    for load in loads:
        load.start()

    barrier = pltpu.get_barrier_semaphore()

    def greet(s, l):
        pl.semaphore_signal(barrier, inc=1, device_id=(s, l), device_id_type=MESH)

    def block_peer(k, kind):
        return lax.rem(x + k, 4) * 4 + other_four(y_lo, core, kind)

    for k, kind in block_peers():
        greet(space, block_peer(k, kind))
    for k in range(1, n_space):
        greet(lax.rem(space + k, n_space), leaf)
    greet(plane, other_y)

    nodes_f[...] = jnp.zeros((3 * PLANE, 128), F32)
    for load in loads[:3]:
        load.wait()
    for c in range(3):
        base = c * PLANE
        value[0:64, 0:RANK] = leaf_nodes[c].astype(F32)
        value[64:72, 0:RANK] = one_nodes[c].astype(F32)
        for h in range(2):
            nodes_f[base : base + 36, h * RANK : (h + 1) * RANK] = value[pl.ds(h, 36, stride=2), 0:RANK]
        nodes_f[base + 36 : base + 37, 0:RANK] = two_nodes[c : c + 1].astype(F32)
    nodes[...] = nodes_f[...].astype(BF16)
    for kind in range(4):
        pieces = []
        for c in range(3):
            base = c * PLANE
            pieces += [
                nodes_f[base + 8 * kind : base + 8 * kind + 8, :],
                nodes_f[base + 32 + kind : base + 33 + kind, :],
                nodes_f[base + 36 : base + 37, :] if kind == 0 else jnp.zeros((1, 128), F32),
                jnp.zeros((6, 128), F32),
            ]
        nodes_t[kind] = jnp.concatenate(pieces, axis=0).astype(BF16)

    def remote(src, dst, send, came, s, l):
        return pltpu.make_async_remote_copy(
            src_ref=src, dst_ref=dst, send_sem=send, recv_sem=came, device_id=(s, l), device_id_type=MESH
        )

    mine = 4 + four
    parts = (None, pl.ds(0, CUT), pl.ds(CUT, 36 - CUT))

    def own(piece):
        return nodes if piece == 0 else coef.at[parts[piece]]

    def held(piece, slot):
        return node_tab.at[slot] if piece == 0 else coef_tab.at[slot, parts[piece]]

    def move(piece, src, slot, send, s, l):
        return remote(src, held(piece, slot), send, recv.at[piece, slot], s, l)

    def own_copies(piece):
        return (
            move(piece, own(piece), 4 + four, send_own.at[piece, 0], space, other_y),
            move(piece, own(piece), far + four, send_own.at[piece, 1], plane, other_y),
            move(piece, own(piece), mine, send_own.at[piece, 2], space, sibling),
        )

    def send_all(piece):
        for copy in own_copies(piece):
            copy.start()

    slot_a, slot_b, slot_c = 4 + four_y, near + four_y, near + four
    slot_z = (far + four_y, far + four)

    def arrived(piece, slot):
        move(piece, held(piece, slot), slot, send_own.at[piece, 0], space, sibling).wait_recv()

    def relay_copy(piece):
        return (
            move(piece, held(piece, slot_a), far + four_y, send_relay.at[piece], plane, other_y),
            move(piece, held(piece, slot_b), near + four_y, send_relay.at[piece], space, other_y),
        )

    def z_copy(piece, which):
        slot = (slot_b, slot_c)[which]
        return move(piece, held(piece, slot), slot_z[which], send_z.at[piece, which], ahead, leaf)

    def sib_copy(piece, which):
        slot = (slot_a, slot_b, slot_c) + slot_z
        return move(piece, held(piece, slot[which]), slot[which], send_sib.at[piece, which], space, sibling)

    def pass_ab(piece):
        by_a, by_b = relay_copy(piece)
        arrived(piece, slot_a)

        @pl.when(core == 0)
        def _():
            by_a.start()

        sib_copy(piece, 0).start()
        arrived(piece, slot_b)

        @pl.when(core == 1)
        def _():
            by_b.start()

        @pl.when(has_ahead)
        def _():
            z_copy(piece, 0).start()

        sib_copy(piece, 1).start()

    def pass_c(piece):
        arrived(piece, slot_c)

        @pl.when(has_ahead)
        def _():
            z_copy(piece, 1).start()

        sib_copy(piece, 2).start()

    def pass_z(piece):
        @pl.when(has_behind)
        def _():
            for which in range(2):
                arrived(piece, slot_z[which])
                sib_copy(piece, 3 + which).start()

    def leaves(i, carry):
        for j in range(4):
            pair = i * 4 + j
            halves = [
                nt(charges[:, pl.ds(pl.multiple_of((2 * pair + h) * 128, 128), 128)], basis[2 * pair + h])
                for h in range(2)
            ]
            coef[pair] = jnp.concatenate(halves, axis=1).astype(BF16)
        return carry

    pl.semaphore_wait(barrier, 15 + (n_space - 1) + 1)
    send_all(0)

    def target_copy(k, kind):
        home = x * 4 + kind
        return remote(
            nodes_t.at[kind], target_nodes.at[home], send_x.at[k * 4 + kind], recv_x.at[home],
            space, block_peer(k, kind),
        )

    for k, kind in block_peers():
        target_copy(k, kind).start()
    loads[3].wait()
    loads[4].wait()
    lax.fori_loop(0, CUT // 4, leaves, 0)
    send_all(1)
    lax.fori_loop(CUT // 4, 8, leaves, 0)

    loads[5].wait()
    for i in range(4):
        halves = []
        for h in range(2):
            p = 2 * i + h
            stacked = jnp.concatenate([coef[4 * p + j] for j in range(4)], axis=1)
            halves.append(nt(stacked, t_one[p]))
        coef[32 + i] = jnp.concatenate(halves, axis=1).astype(BF16)
    loads[6].wait()
    top = nt(jnp.concatenate([coef[32 + j] for j in range(4)], axis=1), t_two[0])
    tx, ty, tz = (nodes_f[c * PLANE + 36 : c * PLANE + 37, 0:RANK] for c in range(3))
    rows = (tx, ty, tz) + split3(tx * tx + ty * ty + tz * tz)
    row = lax.broadcasted_iota(jnp.int32, (16, RANK), 0)
    feature = jnp.where((row >= 6) & (row < 9), 1.0, 0.0)
    for k, part in enumerate(rows):
        feature = jnp.where(row == k, jnp.broadcast_to(part, (16, RANK)), feature)
    entry[...] = jnp.concatenate([feature, top], axis=1).astype(BF16)

    own_two = four * n_space + space

    def two_copy(k):
        return remote(
            entry, two_tab.at[own_two], send_e.at[k], recv_e.at[space],
            lax.rem(space + k, n_space), leaf,
        )

    for k in range(1, n_space):
        two_copy(k).start()
    send_all(2)
    two_tab[own_two] = entry[...]
    pass_ab(0)
    pass_ab(1)

    for load in loads[7:]:
        load.wait()

    def code(links, per_dev, offset):
        owner = links // per_dev
        slot = (owner // 16 - space + 1) * 4 + owner % 4
        coded = owner // 4 % 4 * 1024 + slot * SLOT + offset + links % per_dev
        return jnp.where(links >= 0, coded, 4096)

    packed[0] = jnp.full((ROWS, 128), 4096, jnp.int32)
    leaf_codes = code(leaf_links[...], LEAF_DEV, 0)
    one_codes = code(one_links[...], ONE_DEV, LEAF_DEV)
    for kind in range(4):
        start = kind * CLASS_ROWS
        packed[0, start : start + 16, 0:96] = leaf_codes[16 * kind : 16 * kind + 16]
        packed[0, start + 16 : start + 18, 0:96] = one_codes[2 * kind : 2 * kind + 2]
    two = two_links[...]
    packed[0, 18:19, 0:96] = jnp.where(
        two >= 0, two // 4 % 4 * 1024 + TWO_AT + two % 4 * 16 + two // 16, 4096
    )
    codes = packed[0]
    group = codes // 1024
    before = jnp.where(
        lax.broadcasted_iota(jnp.int32, (128, 128), 0) < lax.broadcasted_iota(jnp.int32, (128, 128), 1), 1.0, 0.0
    ).astype(BF16)
    at = jnp.full((ROWS, 128), -1.0, F32)
    counts = []
    for q in range(4):
        member = jnp.where(group == q, 1.0, 0.0)
        rank = jnp.dot(member.astype(BF16), before, preferred_element_type=F32)
        at = jnp.where(group == q, rank + 128.0 * q, at)
        counts.append(jnp.sum(member, axis=1, keepdims=True))
    order[...] = at
    value[...] = (codes - group * 1024).astype(F32)
    lane = lax.broadcasted_iota(jnp.int32, (8, 128), 1)
    lane_f = lane.astype(F32)
    for q in range(4):
        packed[q] = jnp.broadcast_to(jnp.maximum((counts[q].astype(jnp.int32) + 3) // 4, 1), (ROWS, 128))

    def compact(b, carry):
        block = pl.ds(pl.multiple_of(b * 8, 8), 8)
        where = order[block, :]
        what = value[block, :]
        found = [jnp.full((8, 128), float(ZERO_AT), F32) for _ in range(4)]
        for j in range(96):
            w = jnp.broadcast_to(where[:, j : j + 1], (8, 128))
            v = jnp.broadcast_to(what[:, j : j + 1], (8, 128))
            for q in range(4):
                found[q] = jnp.where(w == lane_f + 128.0 * q, v, found[q])
        for q in range(4):
            packed[q, block, :] = jnp.where(lane == 127, packed[q, block, :], found[q].astype(jnp.int32))
        return carry

    lax.fori_loop(0, 5, compact, 0)
    pass_ab(2)
    lax.fori_loop(5, ROWS // 8, compact, 0)

    def list_copy(k, kind):
        home = x * 4 + kind
        return remote(
            packed.at[lax.rem(x + k, 4), pl.ds(kind * CLASS_ROWS, CLASS_ROWS)], lists.at[home],
            send_l.at[k * 4 + kind], recv_l.at[home], space, block_peer(k, kind),
        )

    for k, kind in block_peers():
        list_copy(k, kind).start()
    keep_list = pltpu.make_async_copy(packed.at[x, pl.ds(0, CLASS_ROWS)], lists.at[x * 4], local_sem)
    keep_list.start()
    pass_c(0)
    pass_c(1)

    def planes(source, size):
        px, py, pz = (source[c * size : (c + 1) * size, :].astype(F32) for c in range(3))
        return px, py, pz, split3(px * px + py * py + pz * pz)

    ones = jnp.ones((PLANE, 128), F32)
    zeros = jnp.zeros((PLANE, 128), F32)
    for k in range(6, 16):
        feat[pl.ds(k, PLANE, stride=16), :] = ones if k < 9 else zeros
    for k in range(3, 16):
        feat_t[pl.ds(k, 16, stride=16), :] = (ones if k < 6 else zeros)[:16]

    def table_copy(slot):
        part = pl.ds(slot * SLOT, SLOT)
        return pltpu.make_async_copy(table.at[part], table_out.at[part], out_sem.at[slot])

    def enter(slot, source, coefs):
        px, py, pz, norm = planes(source, PLANE)
        for k, part in enumerate((px, py, pz) + norm):
            feat[pl.ds(k, PLANE, stride=16), :] = part

        def some(b, carry):
            for j in range(12):
                i = b * 12 + j
                f = feat[pl.ds(pl.multiple_of(i * 16, 16), 16), :].astype(BF16)
                c = coefs(i)
                table[slot * SLOT + 2 * i] = jnp.concatenate([f[:, :RANK], c[:, :RANK]], axis=1)
                table[slot * SLOT + 2 * i + 1] = jnp.concatenate([f[:, RANK:], c[:, RANK:]], axis=1)
            return carry

        lax.fori_loop(0, 3, some, 0)
        table_copy(slot).start()

    def enter_held(slot):
        enter(slot, node_tab.at[slot], lambda i: coef_tab[slot, i])

    def aim(which, source):
        px, py, pz, norm = planes(source, 16)
        for k, part in enumerate((-2.0 * px, -2.0 * py, -2.0 * pz)):
            feat_t[pl.ds(k, 16, stride=16), :] = part
        for k, part in enumerate(norm):
            feat_t[pl.ds(6 + k, 16, stride=16), :] = part

        for b in range(BLOCKS):
            blocks[which * BLOCKS + b] = feat_t[b * 128 : (b + 1) * 128, :].T.astype(BF16)

    enter(mine, nodes, lambda i: coef[i])
    table[pl.ds(ZERO_AT, 8)] = jnp.zeros((8, 16, 128), BF16)
    pass_c(2)
    pass_z(0)
    pass_z(1)

    for k in range(1, n_space):
        source = lax.rem(space + k, n_space)
        remote(
            entry, two_tab.at[four * n_space + source], send_e.at[0], recv_e.at[source], space, leaf
        ).wait_recv()

    def band(which):
        return two_tab.at[pl.ds(which * n_space, n_space)]

    def band_copy(k):
        which, to = ((four, other_y), (four, sibling), (four_y, sibling))[k]
        return remote(band(which), band(which), send_b.at[k], recv_b.at[which], space, to)

    def band_arrived(which):
        remote(band(which), band(which), send_b.at[0], recv_b.at[which], space, sibling).wait_recv()

    band_copy(0).start()
    band_copy(1).start()
    for slot in (slot_a, slot_b):
        enter_held(slot)
    pass_z(2)
    band_arrived(four_y)
    band_copy(2).start()
    aim(x * 4, nodes_t.at[0])
    for k, kind in block_peers():
        home = lax.rem(x + k, 4) * 4 + kind
        remote(nodes_t.at[0], target_nodes.at[home], send_x.at[0], recv_x.at[home], space, leaf).wait_recv()
        aim(home, target_nodes.at[home])
    blocks_copy = pltpu.make_async_copy(blocks, blocks_out, out_sem.at[13])
    blocks_copy.start()
    enter_held(slot_c)

    def from_sibling(slot):
        for piece in range(PIECES):
            arrived(piece, slot)
        enter_held(slot)

    for slot in (4 + beside, 4 + beside_y, near + beside_y, near + beside):
        from_sibling(slot)

    @pl.when(has_behind)
    def _():
        for slot in slot_z:
            enter_held(slot)
        for slot in (far + beside_y, far + beside):
            from_sibling(slot)

    band_arrived(beside)
    band_arrived(beside_y)
    table[pl.ds(TWO_AT, 64)] = two_tab[...]
    rest = pl.ds(TWO_AT, ENTRIES - TWO_AT)
    rest_copy = pltpu.make_async_copy(table.at[rest], table_out.at[rest], out_sem.at[12])
    rest_copy.start()
    for k, kind in block_peers():
        home = lax.rem(x + k, 4) * 4 + kind
        remote(
            packed.at[0, pl.ds(0, CLASS_ROWS)], lists.at[home], send_l.at[0], recv_l.at[home], space, leaf
        ).wait_recv()

    for piece in range(PIECES):
        for copy in own_copies(piece):
            copy.wait_send()
        relay_copy(piece)[0].wait_send()
        for which in range(3):
            sib_copy(piece, which).wait_send()

        @pl.when(has_ahead)
        def _(piece=piece):
            for which in range(2):
                z_copy(piece, which).wait_send()

        @pl.when(has_behind)
        def _(piece=piece):
            for which in range(2):
                sib_copy(piece, 3 + which).wait_send()

    for k in range(1, n_space):
        two_copy(k).wait_send()
    for k in range(3):
        band_copy(k).wait_send()
    for k, kind in block_peers():
        target_copy(k, kind).wait_send()
        list_copy(k, kind).wait_send()
    keep_list.wait()
    for slot in (mine, slot_a, slot_b, slot_c, 4 + beside, 4 + beside_y, near + beside_y, near + beside):
        table_copy(slot).wait()

    @pl.when(has_behind)
    def _():
        for slot in slot_z + (far + beside_y, far + beside):
            table_copy(slot).wait()

    rest_copy.wait()
    blocks_copy.wait()


def upward(n_space, *arrays):
    hbm = pl.BlockSpec(memory_space=pltpu.HBM)
    dma = pltpu.SemaphoreType.DMA
    return pl.pallas_call(
        functools.partial(up_kernel, n_space),
        out_shape=(
            jax.ShapeDtypeStruct((ENTRIES, 16, 128), BF16),
            jax.ShapeDtypeStruct((HOMES * BLOCKS, 128, 128), BF16),
            jax.ShapeDtypeStruct((HOMES, CLASS_ROWS, 128), jnp.int32),
        ),
        in_specs=[hbm] * len(arrays),
        out_specs=[hbm] * 3,
        scratch_shapes=[pltpu.VMEM(a.shape, a.dtype) for a in arrays]
        + [
            pltpu.VMEM((3 * PLANE, 128), F32),
            pltpu.VMEM((3 * PLANE, 128), BF16),
            pltpu.VMEM((4, 48, 128), BF16),
            pltpu.VMEM((PAIRS, 16, 128), BF16),
            pltpu.VMEM((16, 128), BF16),
            pltpu.VMEM((4, ROWS, 128), jnp.int32),
            pltpu.VMEM((ROWS, 128), F32),
            pltpu.VMEM((ROWS, 128), F32),
            pltpu.VMEM((PLANE * 16, 128), F32),
            pltpu.VMEM((256, 128), F32),
            pltpu.VMEM((12, 3 * PLANE, 128), BF16),
            pltpu.VMEM((12, 36, 16, 128), BF16),
            pltpu.VMEM((64, 16, 128), BF16),
            pltpu.VMEM((HOMES, 48, 128), BF16),
            pltpu.VMEM((ENTRIES, 16, 128), BF16),
            pltpu.VMEM((HOMES * BLOCKS, 128, 128), BF16),
            dma((len(arrays),)), dma((14,)),
            dma,
            dma((PIECES, 3)), dma((PIECES,)), dma((PIECES, 2)), dma((PIECES, 5)), dma((PIECES, 12)),
            dma((16,)), dma((16,)),
            dma((3,)), dma((4,)),
            dma((16,)), dma((16,)),
            dma((16,)), dma((16,)),
        ],
        compiler_params=pltpu.CompilerParams(
            collective_id=0, has_side_effects=True, vmem_limit_bytes=VMEM_BYTES
        ),
        name="upward",
    )(*arrays)


def couple_kernel(lists, table_in, blocks_in, out, table, blocks, targets, total, sem):
    loads = (
        pltpu.make_async_copy(blocks_in, blocks, sem.at[0]),
        pltpu.make_async_copy(table_in, table, sem.at[1]),
    )
    for load in loads:
        load.start()

    def clear(i, carry):
        for j in range(16):
            total[i * 16 + j] = jnp.zeros((16, RANK), F32)
        return carry

    lax.fori_loop(0, ALL_ROWS // 16, clear, 0)
    loads[0].wait()

    def spread(q, carry):
        for kind in range(4):
            home = q * 4 + kind
            for i in range(CLASS_PAIRS):
                block = blocks[home * BLOCKS + i // 8]
                start = pl.multiple_of((home * (CLASS_ROWS // 2) + i) * 128, 128)
                at = 16 * (i % 8)
                targets[pl.ds(start, 128), :] = block[:, at : at + 16]
        return carry

    lax.fori_loop(0, 4, spread, 0)
    loads[1].wait()

    end = ALL_ROWS - 1

    def step(carry):
        r, t, g = carry
        for _ in range(UNROLL):
            picked = [table[lists[r, 4 * g + i]] for i in range(4)]
            sources = jnp.concatenate([e[:, :RANK] for e in picked], axis=1)
            coefs = jnp.concatenate([e[:, RANK:] for e in picked], axis=1)
            mine = targets[pl.ds(pl.multiple_of(r * RANK, RANK), RANK), :]
            square = jnp.maximum(jnp.dot(mine, sources, preferred_element_type=F32), 1e-20)
            dist = square * lax.rsqrt(square)
            matrix = ((dist + 1.0 / SCALE) * jnp.exp2(dist * (-SCALE * LOG2E))).astype(BF16)
            total[r] += nt(coefs, matrix)
            done = g + 1 >= lists[r, 127]
            over = t == 18
            r = jnp.where(done, jnp.minimum(jnp.where(over, r + CLASS_ROWS - 18, r + 1), end), r)
            t = jnp.where(done, jnp.where(over, 0, t + 1), t)
            g = jnp.where(done, 0, g + 1)
        return r, t, g

    lax.while_loop(lambda c: c[0] < end, step, (jnp.int32(0), jnp.int32(0), jnp.int32(0)))

    def pack(q, carry):
        for kind in range(4):
            home = q * 4 + kind
            for i in range(CLASS_PAIRS):
                at = home * CLASS_ROWS + 2 * i
                both = jnp.concatenate([total[at], total[at + 1]], axis=1)
                out[home, i] = (both * (AMPLITUDE * SCALE)).astype(BF16)
        return carry

    lax.fori_loop(0, 4, pack, 0)


def coupling(lists, table, blocks):
    hbm = pl.BlockSpec(memory_space=pltpu.HBM)
    return pl.pallas_call(
        couple_kernel,
        grid_spec=pltpu.PrefetchScalarGridSpec(
            num_scalar_prefetch=1,
            grid=(),
            in_specs=[hbm] * 2,
            out_specs=pl.BlockSpec(memory_space=pltpu.VMEM),
            scratch_shapes=[
                pltpu.VMEM((ENTRIES, 16, 128), BF16),
                pltpu.VMEM((HOMES * BLOCKS, 128, 128), BF16),
                pltpu.VMEM((ALL_ROWS * RANK, 16), BF16),
                pltpu.VMEM((ALL_ROWS, 16, RANK), F32),
                pltpu.SemaphoreType.DMA((2,)),
            ],
        ),
        out_shape=jax.ShapeDtypeStruct((HOMES, CLASS_PAIRS, 16, 128), BF16),
        compiler_params=pltpu.CompilerParams(vmem_limit_bytes=VMEM_BYTES),
        name="coupling",
    )(lists, table, blocks)


def down_kernel(
    far, basis_in, t_one_in, t_two_in, out, basis, t_one, t_two, came, near, in_sem, send, recv
):
    space = lax.axis_index("space")
    leaf = lax.axis_index("leaf")
    x = leaf // 4
    four = lax.rem(leaf, 4)
    y_lo = four // 2
    core = lax.rem(four, 2)
    loads = [
        pltpu.make_async_copy(src, dst, in_sem.at[k])
        for k, (src, dst) in enumerate(
            ((t_two_in, t_two), (t_one_in, t_one), (basis_in, basis), (far.at[x * 4], came.at[0, x]))
        )
    ]
    for load in loads:
        load.start()

    def peer(k, kind):
        return lax.rem(x + k, 4) * 4 + other_four(y_lo, core, kind)

    barrier = pltpu.get_barrier_semaphore()
    for k, kind in block_peers():
        pl.semaphore_signal(barrier, inc=1, device_id=(space, peer(k, kind)), device_id_type=MESH)
    pl.semaphore_wait(barrier, 15)

    def copy(k, kind):
        home = lax.rem(x + k, 4) * 4 + kind
        return pltpu.make_async_remote_copy(
            src_ref=far.at[home], dst_ref=came.at[kind, x], send_sem=send.at[k * 4 + kind],
            recv_sem=recv.at[kind * 4 + x], device_id=(space, peer(k, kind)), device_id_type=MESH,
        )

    for k, kind in block_peers():
        copy(k, kind).start()
    for load in loads:
        load.wait()
    for k, kind in block_peers():
        source = lax.rem(x + k, 4)
        pltpu.make_async_remote_copy(
            src_ref=far.at[0], dst_ref=came.at[kind, source], send_sem=send.at[0],
            recv_sem=recv.at[kind * 4 + source], device_id=(space, leaf), device_id_type=MESH,
        ).wait_recv()

    def summed(kind, i):
        return (
            came[kind, 0, i].astype(F32) + came[kind, 1, i].astype(F32)
            + came[kind, 2, i].astype(F32) + came[kind, 3, i].astype(F32)
        )

    local_two = summed(0, 9)[:, :RANK].astype(BF16)
    down_one = jnp.dot(local_two, t_two[0], preferred_element_type=F32)
    for i in range(4):
        near[32 + i] = (summed(i, 8) + down_one[:, 128 * i : 128 * i + 128]).astype(BF16)

    def cluster(i, carry):
        both = near[32 + i]
        for h in range(2):
            local_one = both[:, h * RANK : (h + 1) * RANK]
            down_leaf = jnp.dot(local_one, t_one[2 * i + h], preferred_element_type=F32)
            for j in range(4):
                pair = 8 * i + 4 * h + j
                local_leaf = (summed(i, 4 * h + j) + down_leaf[:, 128 * j : 128 * j + 128]).astype(BF16)
                for s in range(2):
                    at = pl.multiple_of((2 * pair + s) * 128, 128)
                    out[:, pl.ds(at, 128)] = jnp.dot(
                        local_leaf[:, s * RANK : (s + 1) * RANK], basis[2 * pair + s],
                        preferred_element_type=F32,
                    ).astype(BF16)
        return carry

    lax.fori_loop(0, 4, cluster, 0)
    for k, kind in block_peers():
        copy(k, kind).wait_send()


def downward(far, basis, t_one, t_two):
    hbm = pl.BlockSpec(memory_space=pltpu.HBM)
    dma = pltpu.SemaphoreType.DMA
    return pl.pallas_call(
        down_kernel,
        out_shape=jax.ShapeDtypeStruct((16, LEAF_DEV * 128), BF16),
        in_specs=[hbm] * 4,
        out_specs=pl.BlockSpec(memory_space=pltpu.VMEM),
        scratch_shapes=[pltpu.VMEM(a.shape, a.dtype) for a in (basis, t_one, t_two)]
        + [
            pltpu.VMEM((4, 4, CLASS_PAIRS, 16, 128), BF16),
            pltpu.VMEM((36, 16, 128), BF16),
            dma((4,)), dma((16,)), dma((16,)),
        ],
        compiler_params=pltpu.CompilerParams(
            collective_id=1, has_side_effects=True, vmem_limit_bytes=DOWN_BYTES
        ),
        name="downward",
    )(far, basis, t_one, t_two)


def local(
    charges, leaf_basis, transfer_one, transfer_two, nodes_leaf, nodes_one, nodes_two,
    links_leaf, links_one, links_two,
):
    table, blocks, lists = upward(
        lax.axis_size("space"), charges, leaf_basis, transfer_one, transfer_two,
        nodes_leaf.transpose(1, 0, 2), nodes_one.transpose(1, 0, 2), nodes_two.reshape(3, RANK),
        links_leaf, links_one, links_two,
    )
    far = coupling(lists.reshape(ALL_ROWS, 128), table, blocks)
    return downward(far, leaf_basis, transfer_one, transfer_two)


def solution(mesh):
    return jax.shard_map(
        local,
        mesh=mesh,
        in_specs=(
            P(None, ("space", "leaf")),
            P(("space", "leaf"), None, None),
            P(("space", "leaf"), None, None),
            P(("space", "leaf"), None, None),
            P(("space", "leaf"), None, None),
            P(("space", "leaf"), None, None),
            P(("space", "leaf"), None, None),
            P(("space", "leaf"), None),
            P(("space", "leaf"), None),
            P(("space", "leaf"), None),
        ),
        out_specs=P(None, ("space", "leaf")),
        check_vma=False,
    )
```

```python
import functools

import jax
import jax.numpy as jnp
from jax import lax
from jax.experimental import pallas as pl
from jax.experimental.pallas import tpu as pltpu
from jax.sharding import PartitionSpec as P

SCALE = 1.7320508075688772 / 2.0
AMPLITUDE = 0.25
LOG2E = 1.4426950408889634
MESH = pl.DeviceIdType.MESH
F32 = jnp.float32
BF16 = jnp.bfloat16

RANK = 64
LEAF_DEV = 64
ONE_DEV = 8
PAIRS = 37
PLANE = 48
ROWS = 80
SLOT = 72
TWO_AT = 12 * SLOT
ZERO_AT = TWO_AT + 64
ENTRIES = ZERO_AT + 8
UNROLL = 112

PIECES = 3
CUT = 16
BLOCKS = 5
VMEM_BYTES = 58 * 1024 * 1024
DOWN_BYTES = 53 * 1024 * 1024 + 512 * 1024


def nt(a, b):
    return lax.dot_general(a, b, (((1,), (1,)), ((), ())), preferred_element_type=F32)


def split3(value):
    first = value.astype(BF16).astype(F32)
    rest = value - first
    second = rest.astype(BF16).astype(F32)
    return first, second, rest - second


def up_kernel(
    n_space,
    charges_in, basis_in, t_one_in, t_two_in, leaf_nodes_in, one_nodes_in, two_nodes_in,
    leaf_links_in, one_links_in, two_links_in,
    table_out, blocks_out, lists,
    charges, basis, t_one, t_two, leaf_nodes, one_nodes, two_nodes, leaf_links, one_links, two_links,
    nodes_f, nodes, coef, entry, packed, order, value, feat, feat_t,
    node_tab, coef_tab, two_tab, target_nodes, table, blocks,
    in_sem, out_sem, local_sem, send_own, send_relay, send_z, send_sib, recv,
    send_e, recv_e, send_b, recv_b, send_x, recv_x, send_l, recv_l,
):
    space = lax.axis_index("space")
    leaf = lax.axis_index("leaf")
    x = leaf // 4
    four = lax.rem(leaf, 4)
    y_lo = four // 2
    core = lax.rem(four, 2)
    four_y = (1 - y_lo) * 2 + core
    beside = y_lo * 2 + (1 - core)
    beside_y = (1 - y_lo) * 2 + (1 - core)
    other_y = x * 4 + four_y
    sibling = x * 4 + beside
    side = 1 - 2 * lax.rem(space, 2)
    plane = space + side
    ahead = space + 2 * side
    behind = space - 2 * side
    has_ahead = (ahead >= 0) & (ahead < n_space)
    has_behind = (behind >= 0) & (behind < n_space)
    near, far = (1 + side) * 4, (1 - side) * 4

    loads = [
        pltpu.make_async_copy(src, dst, in_sem.at[k])
        for k, (src, dst) in enumerate(
            (
                (leaf_nodes_in, leaf_nodes), (one_nodes_in, one_nodes), (two_nodes_in, two_nodes),
                (charges_in, charges), (basis_in, basis), (t_one_in, t_one), (t_two_in, t_two),
                (leaf_links_in, leaf_links), (one_links_in, one_links), (two_links_in, two_links),
            )
        )
    ]
    for load in loads:
        load.start()

    barrier = pltpu.get_barrier_semaphore()

    def greet(s, l):
        pl.semaphore_signal(barrier, inc=1, device_id=(s, l), device_id_type=MESH)

    for k in range(1, 4):
        greet(space, lax.rem(x + k, 4) * 4 + four)
    for k in range(1, n_space):
        greet(lax.rem(space + k, n_space), leaf)
    greet(space, other_y)
    greet(plane, other_y)
    greet(space, sibling)

    nodes_f[...] = jnp.zeros((3 * PLANE, 128), F32)
    for load in loads[:3]:
        load.wait()
    for c in range(3):
        base = c * PLANE
        value[0:64, 0:RANK] = leaf_nodes[c].astype(F32)
        value[64:72, 0:RANK] = one_nodes[c].astype(F32)
        for h in range(2):
            nodes_f[base : base + 36, h * RANK : (h + 1) * RANK] = value[pl.ds(h, 36, stride=2), 0:RANK]
        nodes_f[base + 36 : base + 37, 0:RANK] = two_nodes[c : c + 1].astype(F32)
    nodes[...] = nodes_f[...].astype(BF16)

    def remote(src, dst, send, came, s, l):
        return pltpu.make_async_remote_copy(
            src_ref=src, dst_ref=dst, send_sem=send, recv_sem=came, device_id=(s, l), device_id_type=MESH
        )

    mine = 4 + four
    parts = (None, pl.ds(0, CUT), pl.ds(CUT, 36 - CUT))

    def own(piece):
        return nodes if piece == 0 else coef.at[parts[piece]]

    def held(piece, slot):
        return node_tab.at[slot] if piece == 0 else coef_tab.at[slot, parts[piece]]

    def move(piece, src, slot, send, s, l):
        return remote(src, held(piece, slot), send, recv.at[piece, slot], s, l)

    def own_copies(piece):
        return (
            move(piece, own(piece), 4 + four, send_own.at[piece, 0], space, other_y),
            move(piece, own(piece), far + four, send_own.at[piece, 1], plane, other_y),
            move(piece, own(piece), mine, send_own.at[piece, 2], space, sibling),
        )

    def send_all(piece):
        for copy in own_copies(piece):
            copy.start()

    slot_a, slot_b, slot_c = 4 + four_y, near + four_y, near + four
    slot_z = (far + four_y, far + four)

    def arrived(piece, slot):
        move(piece, held(piece, slot), slot, send_own.at[piece, 0], space, sibling).wait_recv()

    def relay_copy(piece):
        return (
            move(piece, held(piece, slot_a), far + four_y, send_relay.at[piece], plane, other_y),
            move(piece, held(piece, slot_b), near + four_y, send_relay.at[piece], space, other_y),
        )

    def z_copy(piece, which):
        slot = (slot_b, slot_c)[which]
        return move(piece, held(piece, slot), slot_z[which], send_z.at[piece, which], ahead, leaf)

    def sib_copy(piece, which):
        slot = (slot_a, slot_b, slot_c) + slot_z
        return move(piece, held(piece, slot[which]), slot[which], send_sib.at[piece, which], space, sibling)

    def pass_ab(piece):
        by_a, by_b = relay_copy(piece)
        arrived(piece, slot_a)

        @pl.when(core == 0)
        def _():
            by_a.start()

        sib_copy(piece, 0).start()
        arrived(piece, slot_b)

        @pl.when(core == 1)
        def _():
            by_b.start()

        @pl.when(has_ahead)
        def _():
            z_copy(piece, 0).start()

        sib_copy(piece, 1).start()

    def pass_c(piece):
        arrived(piece, slot_c)

        @pl.when(has_ahead)
        def _():
            z_copy(piece, 1).start()

        sib_copy(piece, 2).start()

    def pass_z(piece):
        @pl.when(has_behind)
        def _():
            for which in range(2):
                arrived(piece, slot_z[which])
                sib_copy(piece, 3 + which).start()

    def leaves(i, carry):
        for j in range(4):
            pair = i * 4 + j
            halves = [
                nt(charges[:, pl.ds(pl.multiple_of((2 * pair + h) * 128, 128), 128)], basis[2 * pair + h])
                for h in range(2)
            ]
            coef[pair] = jnp.concatenate(halves, axis=1).astype(BF16)
        return carry

    pl.semaphore_wait(barrier, 3 + (n_space - 1) + 3)
    send_all(0)
    for k in range(1, 4):
        to = lax.rem(x + k, 4) * 4 + four
        remote(nodes, target_nodes.at[x], send_x.at[k], recv_x.at[x], space, to).start()
    loads[3].wait()
    loads[4].wait()
    lax.fori_loop(0, CUT // 4, leaves, 0)
    send_all(1)
    lax.fori_loop(CUT // 4, 8, leaves, 0)

    loads[5].wait()
    for i in range(4):
        halves = []
        for h in range(2):
            p = 2 * i + h
            stacked = jnp.concatenate([coef[4 * p + j] for j in range(4)], axis=1)
            halves.append(nt(stacked, t_one[p]))
        coef[32 + i] = jnp.concatenate(halves, axis=1).astype(BF16)
    loads[6].wait()
    top = nt(jnp.concatenate([coef[32 + j] for j in range(4)], axis=1), t_two[0])
    tx, ty, tz = (nodes_f[c * PLANE + 36 : c * PLANE + 37, 0:RANK] for c in range(3))
    rows = (tx, ty, tz) + split3(tx * tx + ty * ty + tz * tz)
    row = lax.broadcasted_iota(jnp.int32, (16, RANK), 0)
    feature = jnp.where((row >= 6) & (row < 9), 1.0, 0.0)
    for k, part in enumerate(rows):
        feature = jnp.where(row == k, jnp.broadcast_to(part, (16, RANK)), feature)
    entry[...] = jnp.concatenate([feature, top], axis=1).astype(BF16)

    own_two = four * n_space + space

    def two_copy(k):
        return remote(
            entry, two_tab.at[own_two], send_e.at[k], recv_e.at[space],
            lax.rem(space + k, n_space), leaf,
        )

    for k in range(1, n_space):
        two_copy(k).start()
    send_all(2)
    two_tab[own_two] = entry[...]
    pass_ab(0)
    pass_ab(1)

    for load in loads[7:]:
        load.wait()

    def code(links, per_dev, offset):
        owner = links // per_dev
        slot = (owner // 16 - space + 1) * 4 + owner % 4
        coded = owner // 4 % 4 * 1024 + slot * SLOT + offset + links % per_dev
        return jnp.where(links >= 0, coded, 4096)

    packed[0] = jnp.full((ROWS, 128), 4096, jnp.int32)
    packed[0, 0:64, 0:96] = code(leaf_links[...], LEAF_DEV, 0)
    packed[0, 64:72, 0:96] = code(one_links[...], ONE_DEV, LEAF_DEV)
    two = two_links[...]
    packed[0, 72:73, 0:96] = jnp.where(
        two >= 0, two // 4 % 4 * 1024 + TWO_AT + two % 4 * 16 + two // 16, 4096
    )
    codes = packed[0]
    group = codes // 1024
    before = jnp.where(
        lax.broadcasted_iota(jnp.int32, (128, 128), 0) < lax.broadcasted_iota(jnp.int32, (128, 128), 1), 1.0, 0.0
    ).astype(BF16)
    at = jnp.full((ROWS, 128), -1.0, F32)
    counts = []
    for q in range(4):
        member = jnp.where(group == q, 1.0, 0.0)
        rank = jnp.dot(member.astype(BF16), before, preferred_element_type=F32)
        at = jnp.where(group == q, rank + 128.0 * q, at)
        counts.append(jnp.sum(member, axis=1, keepdims=True))
    order[...] = at
    value[...] = (codes - group * 1024).astype(F32)
    lane = lax.broadcasted_iota(jnp.int32, (8, 128), 1)
    lane_f = lane.astype(F32)
    for q in range(4):
        packed[q] = jnp.broadcast_to(jnp.maximum((counts[q].astype(jnp.int32) + 3) // 4, 1), (ROWS, 128))

    def compact(b, carry):
        block = pl.ds(pl.multiple_of(b * 8, 8), 8)
        where = order[block, :]
        what = value[block, :]
        found = [jnp.full((8, 128), float(ZERO_AT), F32) for _ in range(4)]
        for j in range(96):
            w = jnp.broadcast_to(where[:, j : j + 1], (8, 128))
            v = jnp.broadcast_to(what[:, j : j + 1], (8, 128))
            for q in range(4):
                found[q] = jnp.where(w == lane_f + 128.0 * q, v, found[q])
        for q in range(4):
            packed[q, block, :] = jnp.where(lane == 127, packed[q, block, :], found[q].astype(jnp.int32))
        return carry

    lax.fori_loop(0, 4, compact, 0)
    pass_ab(2)
    lax.fori_loop(4, ROWS // 8, compact, 0)
    for k in range(1, 4):
        to = lax.rem(x + k, 4)
        remote(packed.at[to], lists.at[x], send_l.at[k], recv_l.at[x], space, to * 4 + four).start()
    keep_list = pltpu.make_async_copy(packed.at[x], lists.at[x], local_sem)
    keep_list.start()
    pass_c(0)
    pass_c(1)

    def planes(source):
        px, py, pz = (source[c * PLANE : (c + 1) * PLANE, :].astype(F32) for c in range(3))
        return px, py, pz, split3(px * px + py * py + pz * pz)

    ones = jnp.ones((PLANE, 128), F32)
    zeros = jnp.zeros((PLANE, 128), F32)
    for k in range(6, 16):
        feat[pl.ds(k, PLANE, stride=16), :] = ones if k < 9 else zeros
    for k in range(3, 16):
        feat_t[pl.ds(k, PLANE, stride=16), :] = ones if k < 6 else zeros

    def table_copy(slot):
        part = pl.ds(slot * SLOT, SLOT)
        return pltpu.make_async_copy(table.at[part], table_out.at[part], out_sem.at[slot])

    def enter(slot, source, coefs):
        px, py, pz, norm = planes(source)
        for k, part in enumerate((px, py, pz) + norm):
            feat[pl.ds(k, PLANE, stride=16), :] = part

        def some(b, carry):
            for j in range(12):
                i = b * 12 + j
                f = feat[pl.ds(pl.multiple_of(i * 16, 16), 16), :].astype(BF16)
                c = coefs(i)
                table[slot * SLOT + 2 * i] = jnp.concatenate([f[:, :RANK], c[:, :RANK]], axis=1)
                table[slot * SLOT + 2 * i + 1] = jnp.concatenate([f[:, RANK:], c[:, RANK:]], axis=1)
            return carry

        lax.fori_loop(0, 3, some, 0)
        table_copy(slot).start()

    def enter_held(slot):
        enter(slot, node_tab.at[slot], lambda i: coef_tab[slot, i])

    def aim(which, source):
        px, py, pz, norm = planes(source)
        for k, part in enumerate((-2.0 * px, -2.0 * py, -2.0 * pz)):
            feat_t[pl.ds(k, PLANE, stride=16), :] = part
        for k, part in enumerate(norm):
            feat_t[pl.ds(6 + k, PLANE, stride=16), :] = part

        for b in range(BLOCKS):
            blocks[which * BLOCKS + b] = feat_t[b * 128 : (b + 1) * 128, :].T.astype(BF16)

    enter(mine, nodes, lambda i: coef[i])
    table[pl.ds(ZERO_AT, 8)] = jnp.zeros((8, 16, 128), BF16)
    pass_c(2)
    pass_z(0)
    pass_z(1)

    for k in range(1, n_space):
        source = lax.rem(space + k, n_space)
        remote(
            entry, two_tab.at[four * n_space + source], send_e.at[0], recv_e.at[source], space, leaf
        ).wait_recv()

    def band(which):
        return two_tab.at[pl.ds(which * n_space, n_space)]

    def band_copy(k):
        which, to = ((four, other_y), (four, sibling), (four_y, sibling))[k]
        return remote(band(which), band(which), send_b.at[k], recv_b.at[which], space, to)

    def band_arrived(which):
        remote(band(which), band(which), send_b.at[0], recv_b.at[which], space, sibling).wait_recv()

    band_copy(0).start()
    band_copy(1).start()
    for slot in (slot_a, slot_b):
        enter_held(slot)
    pass_z(2)
    band_arrived(four_y)
    band_copy(2).start()
    aim(x, nodes)
    for k in range(1, 4):
        source = lax.rem(x + k, 4)
        remote(nodes, target_nodes.at[source], send_x.at[k], recv_x.at[source], space, leaf).wait_recv()
        aim(source, target_nodes.at[source])
    blocks_copy = pltpu.make_async_copy(blocks, blocks_out, out_sem.at[13])
    blocks_copy.start()
    enter_held(slot_c)

    def from_sibling(slot):
        for piece in range(PIECES):
            arrived(piece, slot)
        enter_held(slot)

    for slot in (4 + beside, 4 + beside_y, near + beside_y, near + beside):
        from_sibling(slot)

    @pl.when(has_behind)
    def _():
        for slot in slot_z:
            enter_held(slot)
        for slot in (far + beside_y, far + beside):
            from_sibling(slot)

    band_arrived(beside)
    band_arrived(beside_y)
    table[pl.ds(TWO_AT, 64)] = two_tab[...]
    rest = pl.ds(TWO_AT, ENTRIES - TWO_AT)
    rest_copy = pltpu.make_async_copy(table.at[rest], table_out.at[rest], out_sem.at[12])
    rest_copy.start()
    for k in range(1, 4):
        source = lax.rem(x + k, 4)
        remote(packed.at[0], lists.at[source], send_l.at[k], recv_l.at[source], space, leaf).wait_recv()

    for piece in range(PIECES):
        for copy in own_copies(piece):
            copy.wait_send()
        relay_copy(piece)[0].wait_send()
        for which in range(3):
            sib_copy(piece, which).wait_send()

        @pl.when(has_ahead)
        def _(piece=piece):
            for which in range(2):
                z_copy(piece, which).wait_send()

        @pl.when(has_behind)
        def _(piece=piece):
            for which in range(2):
                sib_copy(piece, 3 + which).wait_send()

    for k in range(1, n_space):
        two_copy(k).wait_send()
    for k in range(3):
        band_copy(k).wait_send()
    for k in range(1, 4):
        to = lax.rem(x + k, 4)
        remote(nodes, target_nodes.at[x], send_x.at[k], recv_x.at[x], space, to * 4 + four).wait_send()
        remote(packed.at[to], lists.at[x], send_l.at[k], recv_l.at[x], space, to * 4 + four).wait_send()
    keep_list.wait()
    for slot in (mine, slot_a, slot_b, slot_c, 4 + beside, 4 + beside_y, near + beside_y, near + beside):
        table_copy(slot).wait()

    @pl.when(has_behind)
    def _():
        for slot in slot_z + (far + beside_y, far + beside):
            table_copy(slot).wait()

    rest_copy.wait()
    blocks_copy.wait()


def upward(n_space, *arrays):
    hbm = pl.BlockSpec(memory_space=pltpu.HBM)
    dma = pltpu.SemaphoreType.DMA
    return pl.pallas_call(
        functools.partial(up_kernel, n_space),
        out_shape=(
            jax.ShapeDtypeStruct((ENTRIES, 16, 128), BF16),
            jax.ShapeDtypeStruct((4 * BLOCKS, 128, 128), BF16),
            jax.ShapeDtypeStruct((4, ROWS, 128), jnp.int32),
        ),
        in_specs=[hbm] * len(arrays),
        out_specs=[hbm] * 3,
        scratch_shapes=[pltpu.VMEM(a.shape, a.dtype) for a in arrays]
        + [
            pltpu.VMEM((3 * PLANE, 128), F32),
            pltpu.VMEM((3 * PLANE, 128), BF16),
            pltpu.VMEM((PAIRS, 16, 128), BF16),
            pltpu.VMEM((16, 128), BF16),
            pltpu.VMEM((4, ROWS, 128), jnp.int32),
            pltpu.VMEM((ROWS, 128), F32),
            pltpu.VMEM((ROWS, 128), F32),
            pltpu.VMEM((PLANE * 16, 128), F32),
            pltpu.VMEM((PLANE * 16, 128), F32),
            pltpu.VMEM((12, 3 * PLANE, 128), BF16),
            pltpu.VMEM((12, 36, 16, 128), BF16),
            pltpu.VMEM((64, 16, 128), BF16),
            pltpu.VMEM((4, 3 * PLANE, 128), BF16),
            pltpu.VMEM((ENTRIES, 16, 128), BF16),
            pltpu.VMEM((4 * BLOCKS, 128, 128), BF16),
            dma((len(arrays),)), dma((14,)),
            dma,
            dma((PIECES, 3)), dma((PIECES,)), dma((PIECES, 2)), dma((PIECES, 5)), dma((PIECES, 12)),
            dma((16,)), dma((16,)),
            dma((3,)), dma((4,)),
            dma((4,)), dma((4,)),
            dma((4,)), dma((4,)),
        ],
        compiler_params=pltpu.CompilerParams(
            collective_id=0, has_side_effects=True, vmem_limit_bytes=VMEM_BYTES
        ),
        name="upward",
    )(*arrays)


def couple_kernel(
    lists_in, table_in, blocks_in, out, lists, table, blocks, targets, total, sem
):
    loads = (
        pltpu.make_async_copy(blocks_in, blocks, sem.at[0]),
        pltpu.make_async_copy(table_in, table, sem.at[1]),
        pltpu.make_async_copy(lists_in, lists, sem.at[2]),
    )
    for load in loads:
        load.start()

    def clear(i, carry):
        for j in range(16):
            total[i * 16 + j] = jnp.zeros((16, RANK), F32)
        return carry

    lax.fori_loop(0, 4 * ROWS // 16, clear, 0)
    loads[0].wait()

    def spread(q, carry):
        for i in range(BLOCKS):
            block = blocks[q * BLOCKS + i]
            for j in range(8):
                start = pl.multiple_of(((q * BLOCKS + i) * 8 + j) * 128, 128)
                targets[pl.ds(start, 128), :] = block[:, 16 * j : 16 * j + 16]
        return carry

    lax.fori_loop(0, 4, spread, 0)
    loads[1].wait()
    loads[2].wait()

    end = 4 * ROWS - 1

    def step(carry):
        r, t, g = carry
        for _ in range(UNROLL):
            picked = [table[lists[r, 4 * g + i]] for i in range(4)]
            sources = jnp.concatenate([e[:, :RANK] for e in picked], axis=1)
            coefs = jnp.concatenate([e[:, RANK:] for e in picked], axis=1)
            mine = targets[pl.ds(pl.multiple_of(r * RANK, RANK), RANK), :]
            square = jnp.maximum(jnp.dot(mine, sources, preferred_element_type=F32), 1e-20)
            dist = square * lax.rsqrt(square)
            matrix = ((dist + 1.0 / SCALE) * jnp.exp2(dist * (-SCALE * LOG2E))).astype(BF16)
            total[r] += nt(coefs, matrix)
            done = g + 1 >= lists[r, 127]
            over = t == 72
            r = jnp.where(done, jnp.minimum(jnp.where(over, r + 8, r + 1), end), r)
            t = jnp.where(done, jnp.where(over, 0, t + 1), t)
            g = jnp.where(done, 0, g + 1)
        return r, t, g

    lax.while_loop(lambda c: c[0] < end, step, (jnp.int32(0), jnp.int32(0), jnp.int32(0)))

    def pack(q, carry):
        for i in range(PAIRS):
            at = q * ROWS + 2 * i
            both = jnp.concatenate([total[at], total[at + 1]], axis=1)
            out[q, i] = (both * (AMPLITUDE * SCALE)).astype(BF16)
        return carry

    lax.fori_loop(0, 4, pack, 0)


def coupling(lists, table, blocks):
    hbm = pl.BlockSpec(memory_space=pltpu.HBM)
    return pl.pallas_call(
        couple_kernel,
        in_specs=[hbm] * 3,
        out_specs=pl.BlockSpec(memory_space=pltpu.VMEM),
        scratch_shapes=[
            pltpu.SMEM((4 * ROWS, 128), jnp.int32),
            pltpu.VMEM((ENTRIES, 16, 128), BF16),
            pltpu.VMEM((4 * BLOCKS, 128, 128), BF16),
            pltpu.VMEM((4 * ROWS * RANK, 16), BF16),
            pltpu.VMEM((4 * ROWS, 16, RANK), F32),
            pltpu.SemaphoreType.DMA((3,)),
        ],
        out_shape=jax.ShapeDtypeStruct((4, PAIRS, 16, 128), BF16),
        compiler_params=pltpu.CompilerParams(vmem_limit_bytes=VMEM_BYTES),
        name="coupling",
    )(lists, table, blocks)


def down_kernel(
    far, basis_in, t_one_in, t_two_in, out, basis, t_one, t_two, came, near, in_sem, send, recv
):
    space = lax.axis_index("space")
    leaf = lax.axis_index("leaf")
    x = leaf // 4
    four = lax.rem(leaf, 4)
    loads = [
        pltpu.make_async_copy(src, dst, in_sem.at[k])
        for k, (src, dst) in enumerate(((t_two_in, t_two), (t_one_in, t_one), (basis_in, basis), (far.at[x], came.at[x])))
    ]
    for load in loads:
        load.start()
    barrier = pltpu.get_barrier_semaphore()
    for k in range(1, 4):
        to = lax.rem(x + k, 4) * 4 + four
        pl.semaphore_signal(barrier, inc=1, device_id=(space, to), device_id_type=MESH)
    pl.semaphore_wait(barrier, 3)

    def copy(k):
        to = lax.rem(x + k, 4)
        return pltpu.make_async_remote_copy(
            src_ref=far.at[to], dst_ref=came.at[x], send_sem=send.at[k], recv_sem=recv.at[x],
            device_id=(space, to * 4 + four), device_id_type=MESH,
        )

    for k in range(1, 4):
        copy(k).start()
    for load in loads:
        load.wait()
    for k in range(1, 4):
        source = lax.rem(x + k, 4)
        pltpu.make_async_remote_copy(
            src_ref=far.at[source], dst_ref=came.at[source], send_sem=send.at[k], recv_sem=recv.at[source],
            device_id=(space, leaf), device_id_type=MESH,
        ).wait_recv()

    def summed(i):
        return (
            came[0, i].astype(F32) + came[1, i].astype(F32)
            + came[2, i].astype(F32) + came[3, i].astype(F32)
        )

    local_two = summed(36)[:, :RANK].astype(BF16)
    down_one = jnp.dot(local_two, t_two[0], preferred_element_type=F32)
    for i in range(4):
        near[32 + i] = (summed(32 + i) + down_one[:, 128 * i : 128 * i + 128]).astype(BF16)

    def cluster(i, carry):
        both = near[32 + i]
        for h in range(2):
            local_one = both[:, h * RANK : (h + 1) * RANK]
            down_leaf = jnp.dot(local_one, t_one[2 * i + h], preferred_element_type=F32)
            for j in range(4):
                pair = 8 * i + 4 * h + j
                local_leaf = (summed(pair) + down_leaf[:, 128 * j : 128 * j + 128]).astype(BF16)
                for s in range(2):
                    at = pl.multiple_of((2 * pair + s) * 128, 128)
                    out[:, pl.ds(at, 128)] = jnp.dot(
                        local_leaf[:, s * RANK : (s + 1) * RANK], basis[2 * pair + s],
                        preferred_element_type=F32,
                    ).astype(BF16)
        return carry

    lax.fori_loop(0, 4, cluster, 0)
    for k in range(1, 4):
        copy(k).wait_send()


def downward(far, basis, t_one, t_two):
    hbm = pl.BlockSpec(memory_space=pltpu.HBM)
    dma = pltpu.SemaphoreType.DMA
    return pl.pallas_call(
        down_kernel,
        out_shape=jax.ShapeDtypeStruct((16, LEAF_DEV * 128), BF16),
        in_specs=[hbm] * 4,
        out_specs=pl.BlockSpec(memory_space=pltpu.VMEM),
        scratch_shapes=[pltpu.VMEM(a.shape, a.dtype) for a in (basis, t_one, t_two)]
        + [
            pltpu.VMEM((4, PAIRS, 16, 128), BF16),
            pltpu.VMEM((36, 16, 128), BF16),
            dma((4,)), dma((4,)), dma((4,)),
        ],
        compiler_params=pltpu.CompilerParams(
            collective_id=1, has_side_effects=True, vmem_limit_bytes=DOWN_BYTES
        ),
        name="downward",
    )(far, basis, t_one, t_two)


def local(
    charges, leaf_basis, transfer_one, transfer_two, nodes_leaf, nodes_one, nodes_two,
    links_leaf, links_one, links_two,
):
    table, blocks, lists = upward(
        lax.axis_size("space"), charges, leaf_basis, transfer_one, transfer_two,
        nodes_leaf.transpose(1, 0, 2), nodes_one.transpose(1, 0, 2), nodes_two.reshape(3, RANK),
        links_leaf, links_one, links_two,
    )
    far = coupling(lists.reshape(4 * ROWS, 128), table, blocks)
    return downward(far, leaf_basis, transfer_one, transfer_two)


def solution(mesh):
    return jax.shard_map(
        local,
        mesh=mesh,
        in_specs=(
            P(None, ("space", "leaf")),
            P(("space", "leaf"), None, None),
            P(("space", "leaf"), None, None),
            P(("space", "leaf"), None, None),
            P(("space", "leaf"), None, None),
            P(("space", "leaf"), None, None),
            P(("space", "leaf"), None, None),
            P(("space", "leaf"), None),
            P(("space", "leaf"), None),
            P(("space", "leaf"), None),
        ),
        out_specs=P(None, ("space", "leaf")),
        check_vma=False,
    )
```

```python
import functools

import jax
import jax.numpy as jnp
from jax import lax
from jax.experimental import pallas as pl
from jax.experimental.pallas import tpu as pltpu
from jax.sharding import PartitionSpec as P

SCALE = 1.7320508075688772 / 2.0
AMPLITUDE = 0.25
LOG2E = 1.4426950408889634
MESH = pl.DeviceIdType.MESH
F32 = jnp.float32
BF16 = jnp.bfloat16

RANK = 64
LEAF_DEV = 64
ONE_DEV = 8
PAIRS = 37
PLANE = 48
ROWS = 80
SLOT = 72
TWO_AT = 12 * SLOT
ZERO_AT = TWO_AT + 64
ENTRIES = ZERO_AT + 8
UNROLL = 112

PIECES = 3
CUT = 16
BLOCKS = 5
VMEM_BYTES = 58 * 1024 * 1024
DOWN_PARTS = ((32, 5), (0, 8), (8, 8), (16, 8), (24, 8))
DOWN_BYTES = 53 * 1024 * 1024 + 512 * 1024


def nt(a, b):
    return lax.dot_general(a, b, (((1,), (1,)), ((), ())), preferred_element_type=F32)


def split3(value):
    first = value.astype(BF16).astype(F32)
    rest = value - first
    second = rest.astype(BF16).astype(F32)
    return first, second, rest - second


def up_kernel(
    n_space,
    charges_in, basis_in, t_one_in, t_two_in, leaf_nodes_in, one_nodes_in, two_nodes_in,
    leaf_links_in, one_links_in, two_links_in,
    table_out, blocks_out, lists,
    charges, basis, t_one, t_two, leaf_nodes, one_nodes, two_nodes, leaf_links, one_links, two_links,
    nodes_f, nodes, coef, entry, packed, order, value, feat, feat_t,
    node_tab, coef_tab, two_tab, target_nodes, table, blocks,
    in_sem, out_sem, local_sem, send_own, send_relay, send_z, send_sib, recv,
    send_e, recv_e, send_b, recv_b, send_x, recv_x, send_l, recv_l,
):
    space = lax.axis_index("space")
    leaf = lax.axis_index("leaf")
    x = leaf // 4
    four = lax.rem(leaf, 4)
    y_lo = four // 2
    core = lax.rem(four, 2)
    four_y = (1 - y_lo) * 2 + core
    beside = y_lo * 2 + (1 - core)
    beside_y = (1 - y_lo) * 2 + (1 - core)
    other_y = x * 4 + four_y
    sibling = x * 4 + beside
    side = 1 - 2 * lax.rem(space, 2)
    plane = space + side
    ahead = space + 2 * side
    behind = space - 2 * side
    has_ahead = (ahead >= 0) & (ahead < n_space)
    has_behind = (behind >= 0) & (behind < n_space)
    near, far = (1 + side) * 4, (1 - side) * 4

    loads = [
        pltpu.make_async_copy(src, dst, in_sem.at[k])
        for k, (src, dst) in enumerate(
            (
                (leaf_nodes_in, leaf_nodes), (one_nodes_in, one_nodes), (two_nodes_in, two_nodes),
                (charges_in, charges), (basis_in, basis), (t_one_in, t_one), (t_two_in, t_two),
                (leaf_links_in, leaf_links), (one_links_in, one_links), (two_links_in, two_links),
            )
        )
    ]
    for load in loads:
        load.start()

    barrier = pltpu.get_barrier_semaphore()

    def greet(s, l):
        pl.semaphore_signal(barrier, inc=1, device_id=(s, l), device_id_type=MESH)

    for k in range(1, 4):
        greet(space, lax.rem(x + k, 4) * 4 + four)
    for k in range(1, n_space):
        greet(lax.rem(space + k, n_space), leaf)
    greet(space, other_y)
    greet(plane, other_y)
    greet(space, sibling)

    nodes_f[...] = jnp.zeros((3 * PLANE, 128), F32)
    for load in loads[:3]:
        load.wait()
    for c in range(3):
        base = c * PLANE
        value[0:64, 0:RANK] = leaf_nodes[c].astype(F32)
        value[64:72, 0:RANK] = one_nodes[c].astype(F32)
        for h in range(2):
            nodes_f[base : base + 36, h * RANK : (h + 1) * RANK] = value[pl.ds(h, 36, stride=2), 0:RANK]
        nodes_f[base + 36 : base + 37, 0:RANK] = two_nodes[c : c + 1].astype(F32)
    nodes[...] = nodes_f[...].astype(BF16)

    def remote(src, dst, send, came, s, l):
        return pltpu.make_async_remote_copy(
            src_ref=src, dst_ref=dst, send_sem=send, recv_sem=came, device_id=(s, l), device_id_type=MESH
        )

    mine = 4 + four
    parts = (None, pl.ds(0, CUT), pl.ds(CUT, 36 - CUT))

    def own(piece):
        return nodes if piece == 0 else coef.at[parts[piece]]

    def held(piece, slot):
        return node_tab.at[slot] if piece == 0 else coef_tab.at[slot, parts[piece]]

    def move(piece, src, slot, send, s, l):
        return remote(src, held(piece, slot), send, recv.at[piece, slot], s, l)

    def own_copies(piece):
        return (
            move(piece, own(piece), 4 + four, send_own.at[piece, 0], space, other_y),
            move(piece, own(piece), far + four, send_own.at[piece, 1], plane, other_y),
            move(piece, own(piece), mine, send_own.at[piece, 2], space, sibling),
        )

    def send_all(piece):
        for copy in own_copies(piece):
            copy.start()

    slot_a, slot_b, slot_c = 4 + four_y, near + four_y, near + four
    slot_z = (far + four_y, far + four)

    def arrived(piece, slot):
        move(piece, held(piece, slot), slot, send_own.at[piece, 0], space, sibling).wait_recv()

    def relay_copy(piece):
        return (
            move(piece, held(piece, slot_a), far + four_y, send_relay.at[piece], plane, other_y),
            move(piece, held(piece, slot_b), near + four_y, send_relay.at[piece], space, other_y),
        )

    def z_copy(piece, which):
        slot = (slot_b, slot_c)[which]
        return move(piece, held(piece, slot), slot_z[which], send_z.at[piece, which], ahead, leaf)

    def sib_copy(piece, which):
        slot = (slot_a, slot_b, slot_c) + slot_z
        return move(piece, held(piece, slot[which]), slot[which], send_sib.at[piece, which], space, sibling)

    def pass_ab(piece):
        by_a, by_b = relay_copy(piece)
        arrived(piece, slot_a)

        @pl.when(core == 0)
        def _():
            by_a.start()

        sib_copy(piece, 0).start()
        arrived(piece, slot_b)

        @pl.when(core == 1)
        def _():
            by_b.start()

        @pl.when(has_ahead)
        def _():
            z_copy(piece, 0).start()

        sib_copy(piece, 1).start()

    def pass_c(piece):
        arrived(piece, slot_c)

        @pl.when(has_ahead)
        def _():
            z_copy(piece, 1).start()

        sib_copy(piece, 2).start()

    def pass_z(piece):
        @pl.when(has_behind)
        def _():
            for which in range(2):
                arrived(piece, slot_z[which])
                sib_copy(piece, 3 + which).start()

    def leaves(i, carry):
        for j in range(4):
            pair = i * 4 + j
            halves = [
                nt(charges[:, pl.ds(pl.multiple_of((2 * pair + h) * 128, 128), 128)], basis[2 * pair + h])
                for h in range(2)
            ]
            coef[pair] = jnp.concatenate(halves, axis=1).astype(BF16)
        return carry

    pl.semaphore_wait(barrier, 3 + (n_space - 1) + 3)
    send_all(0)
    for k in range(1, 4):
        to = lax.rem(x + k, 4) * 4 + four
        remote(nodes, target_nodes.at[x], send_x.at[k], recv_x.at[x], space, to).start()
    loads[3].wait()
    loads[4].wait()
    lax.fori_loop(0, CUT // 4, leaves, 0)
    send_all(1)
    lax.fori_loop(CUT // 4, 8, leaves, 0)

    loads[5].wait()
    for i in range(4):
        halves = []
        for h in range(2):
            p = 2 * i + h
            stacked = jnp.concatenate([coef[4 * p + j] for j in range(4)], axis=1)
            halves.append(nt(stacked, t_one[p]))
        coef[32 + i] = jnp.concatenate(halves, axis=1).astype(BF16)
    loads[6].wait()
    top = nt(jnp.concatenate([coef[32 + j] for j in range(4)], axis=1), t_two[0])
    tx, ty, tz = (nodes_f[c * PLANE + 36 : c * PLANE + 37, 0:RANK] for c in range(3))
    rows = (tx, ty, tz) + split3(tx * tx + ty * ty + tz * tz)
    row = lax.broadcasted_iota(jnp.int32, (16, RANK), 0)
    feature = jnp.where((row >= 6) & (row < 9), 1.0, 0.0)
    for k, part in enumerate(rows):
        feature = jnp.where(row == k, jnp.broadcast_to(part, (16, RANK)), feature)
    entry[...] = jnp.concatenate([feature, top], axis=1).astype(BF16)

    own_two = four * n_space + space

    def two_copy(k):
        return remote(
            entry, two_tab.at[own_two], send_e.at[k], recv_e.at[space],
            lax.rem(space + k, n_space), leaf,
        )

    for k in range(1, n_space):
        two_copy(k).start()
    send_all(2)
    two_tab[own_two] = entry[...]
    pass_ab(0)
    pass_ab(1)

    for load in loads[7:]:
        load.wait()

    def code(links, per_dev, offset):
        owner = links // per_dev
        slot = (owner // 16 - space + 1) * 4 + owner % 4
        coded = owner // 4 % 4 * 1024 + slot * SLOT + offset + links % per_dev
        return jnp.where(links >= 0, coded, 4096)

    packed[0] = jnp.full((ROWS, 128), 4096, jnp.int32)
    packed[0, 0:64, 0:96] = code(leaf_links[...], LEAF_DEV, 0)
    packed[0, 64:72, 0:96] = code(one_links[...], ONE_DEV, LEAF_DEV)
    two = two_links[...]
    packed[0, 72:73, 0:96] = jnp.where(
        two >= 0, two // 4 % 4 * 1024 + TWO_AT + two % 4 * 16 + two // 16, 4096
    )
    codes = packed[0]
    group = codes // 1024
    before = jnp.where(
        lax.broadcasted_iota(jnp.int32, (128, 128), 0) < lax.broadcasted_iota(jnp.int32, (128, 128), 1), 1.0, 0.0
    ).astype(BF16)
    at = jnp.full((ROWS, 128), -1.0, F32)
    counts = []
    for q in range(4):
        member = jnp.where(group == q, 1.0, 0.0)
        rank = jnp.dot(member.astype(BF16), before, preferred_element_type=F32)
        at = jnp.where(group == q, rank + 128.0 * q, at)
        counts.append(jnp.sum(member, axis=1, keepdims=True))
    order[...] = at.astype(jnp.int32) * 1024 + (codes - group * 1024)
    lane = lax.broadcasted_iota(jnp.int32, (8, 128), 1)
    for q in range(4):
        packed[q] = jnp.broadcast_to(jnp.maximum((counts[q].astype(jnp.int32) + 3) // 4, 1), (ROWS, 128))

    def compact(b, carry):
        block = pl.ds(pl.multiple_of(b * 8, 8), 8)
        coded = order[block, :]
        found = [jnp.full((8, 128), ZERO_AT, jnp.int32) for _ in range(4)]
        for j in range(96):
            one = jnp.broadcast_to(coded[:, j : j + 1], (8, 128))
            place = one >> 10
            for q in range(4):
                found[q] = jnp.where(place == lane + 128 * q, one, found[q])
        for q in range(4):
            packed[q, block, :] = jnp.where(lane == 127, packed[q, block, :], found[q] & 1023)
        return carry

    lax.fori_loop(0, 4, compact, 0)
    pass_ab(2)
    lax.fori_loop(4, ROWS // 8, compact, 0)
    for k in range(1, 4):
        to = lax.rem(x + k, 4)
        remote(packed.at[to], lists.at[x], send_l.at[k], recv_l.at[x], space, to * 4 + four).start()
    keep_list = pltpu.make_async_copy(packed.at[x], lists.at[x], local_sem)
    keep_list.start()
    pass_c(0)
    pass_c(1)

    def planes(source):
        px, py, pz = (source[c * PLANE : (c + 1) * PLANE, :].astype(F32) for c in range(3))
        return px, py, pz, split3(px * px + py * py + pz * pz)

    ones = jnp.ones((PLANE, 128), F32)
    zeros = jnp.zeros((PLANE, 128), F32)
    for k in range(6, 16):
        feat[pl.ds(k, PLANE, stride=16), :] = ones if k < 9 else zeros
    for k in range(3, 16):
        feat_t[pl.ds(k, PLANE, stride=16), :] = ones if k < 6 else zeros

    def table_copy(slot):
        part = pl.ds(slot * SLOT, SLOT)
        return pltpu.make_async_copy(table.at[part], table_out.at[part], out_sem.at[slot])

    def enter(slot, source, coefs):
        px, py, pz, norm = planes(source)
        for k, part in enumerate((px, py, pz) + norm):
            feat[pl.ds(k, PLANE, stride=16), :] = part

        def some(b, carry):
            for j in range(12):
                i = b * 12 + j
                f = feat[pl.ds(pl.multiple_of(i * 16, 16), 16), :].astype(BF16)
                c = coefs(i)
                table[slot * SLOT + 2 * i] = jnp.concatenate([f[:, :RANK], c[:, :RANK]], axis=1)
                table[slot * SLOT + 2 * i + 1] = jnp.concatenate([f[:, RANK:], c[:, RANK:]], axis=1)
            return carry

        lax.fori_loop(0, 3, some, 0)
        table_copy(slot).start()

    def enter_held(slot):
        enter(slot, node_tab.at[slot], lambda i: coef_tab[slot, i])

    def aim(which, source):
        px, py, pz, norm = planes(source)
        for k, part in enumerate((-2.0 * px, -2.0 * py, -2.0 * pz)):
            feat_t[pl.ds(k, PLANE, stride=16), :] = part
        for k, part in enumerate(norm):
            feat_t[pl.ds(6 + k, PLANE, stride=16), :] = part

        for b in range(BLOCKS):
            blocks[which * BLOCKS + b] = feat_t[b * 128 : (b + 1) * 128, :].T.astype(BF16)

    enter(mine, nodes, lambda i: coef[i])
    table[pl.ds(ZERO_AT, 8)] = jnp.zeros((8, 16, 128), BF16)
    pass_c(2)
    pass_z(0)
    pass_z(1)

    for k in range(1, n_space):
        source = lax.rem(space + k, n_space)
        remote(
            entry, two_tab.at[four * n_space + source], send_e.at[0], recv_e.at[source], space, leaf
        ).wait_recv()

    def band(which):
        return two_tab.at[pl.ds(which * n_space, n_space)]

    def band_copy(k):
        which, to = ((four, other_y), (four, sibling), (four_y, sibling))[k]
        return remote(band(which), band(which), send_b.at[k], recv_b.at[which], space, to)

    def band_arrived(which):
        remote(band(which), band(which), send_b.at[0], recv_b.at[which], space, sibling).wait_recv()

    band_copy(0).start()
    band_copy(1).start()
    for slot in (slot_a, slot_b):
        enter_held(slot)
    pass_z(2)
    band_arrived(four_y)
    band_copy(2).start()
    aim(x, nodes)
    for k in range(1, 4):
        source = lax.rem(x + k, 4)
        remote(nodes, target_nodes.at[source], send_x.at[k], recv_x.at[source], space, leaf).wait_recv()
        aim(source, target_nodes.at[source])
    blocks_copy = pltpu.make_async_copy(blocks, blocks_out, out_sem.at[13])
    blocks_copy.start()
    enter_held(slot_c)

    def from_sibling(slot):
        for piece in range(PIECES):
            arrived(piece, slot)
        enter_held(slot)

    for slot in (4 + beside, 4 + beside_y, near + beside_y, near + beside):
        from_sibling(slot)

    @pl.when(has_behind)
    def _():
        for slot in slot_z:
            enter_held(slot)
        for slot in (far + beside_y, far + beside):
            from_sibling(slot)

    band_arrived(beside)
    band_arrived(beside_y)
    table[pl.ds(TWO_AT, 64)] = two_tab[...]
    rest = pl.ds(TWO_AT, ENTRIES - TWO_AT)
    rest_copy = pltpu.make_async_copy(table.at[rest], table_out.at[rest], out_sem.at[12])
    rest_copy.start()
    for k in range(1, 4):
        source = lax.rem(x + k, 4)
        remote(packed.at[0], lists.at[source], send_l.at[k], recv_l.at[source], space, leaf).wait_recv()

    for piece in range(PIECES):
        for copy in own_copies(piece):
            copy.wait_send()
        relay_copy(piece)[0].wait_send()
        for which in range(3):
            sib_copy(piece, which).wait_send()

        @pl.when(has_ahead)
        def _(piece=piece):
            for which in range(2):
                z_copy(piece, which).wait_send()

        @pl.when(has_behind)
        def _(piece=piece):
            for which in range(2):
                sib_copy(piece, 3 + which).wait_send()

    for k in range(1, n_space):
        two_copy(k).wait_send()
    for k in range(3):
        band_copy(k).wait_send()
    for k in range(1, 4):
        to = lax.rem(x + k, 4)
        remote(nodes, target_nodes.at[x], send_x.at[k], recv_x.at[x], space, to * 4 + four).wait_send()
        remote(packed.at[to], lists.at[x], send_l.at[k], recv_l.at[x], space, to * 4 + four).wait_send()
    keep_list.wait()
    for slot in (mine, slot_a, slot_b, slot_c, 4 + beside, 4 + beside_y, near + beside_y, near + beside):
        table_copy(slot).wait()

    @pl.when(has_behind)
    def _():
        for slot in slot_z + (far + beside_y, far + beside):
            table_copy(slot).wait()

    rest_copy.wait()
    blocks_copy.wait()


def upward(n_space, *arrays):
    hbm = pl.BlockSpec(memory_space=pltpu.HBM)
    dma = pltpu.SemaphoreType.DMA
    return pl.pallas_call(
        functools.partial(up_kernel, n_space),
        out_shape=(
            jax.ShapeDtypeStruct((ENTRIES, 16, 128), BF16),
            jax.ShapeDtypeStruct((4 * BLOCKS, 128, 128), BF16),
            jax.ShapeDtypeStruct((4, ROWS, 128), jnp.int32),
        ),
        in_specs=[hbm] * len(arrays),
        out_specs=[hbm] * 3,
        scratch_shapes=[pltpu.VMEM(a.shape, a.dtype) for a in arrays]
        + [
            pltpu.VMEM((3 * PLANE, 128), F32),
            pltpu.VMEM((3 * PLANE, 128), BF16),
            pltpu.VMEM((PAIRS, 16, 128), BF16),
            pltpu.VMEM((16, 128), BF16),
            pltpu.VMEM((4, ROWS, 128), jnp.int32),
            pltpu.VMEM((ROWS, 128), jnp.int32),
            pltpu.VMEM((ROWS, 128), F32),
            pltpu.VMEM((PLANE * 16, 128), F32),
            pltpu.VMEM((PLANE * 16, 128), F32),
            pltpu.VMEM((12, 3 * PLANE, 128), BF16),
            pltpu.VMEM((12, 36, 16, 128), BF16),
            pltpu.VMEM((64, 16, 128), BF16),
            pltpu.VMEM((4, 3 * PLANE, 128), BF16),
            pltpu.VMEM((ENTRIES, 16, 128), BF16),
            pltpu.VMEM((4 * BLOCKS, 128, 128), BF16),
            dma((len(arrays),)), dma((14,)),
            dma,
            dma((PIECES, 3)), dma((PIECES,)), dma((PIECES, 2)), dma((PIECES, 5)), dma((PIECES, 12)),
            dma((16,)), dma((16,)),
            dma((3,)), dma((4,)),
            dma((4,)), dma((4,)),
            dma((4,)), dma((4,)),
        ],
        compiler_params=pltpu.CompilerParams(
            collective_id=0, has_side_effects=True, vmem_limit_bytes=VMEM_BYTES
        ),
        name="upward",
    )(*arrays)


def couple_kernel(
    lists_in, table_in, blocks_in, out, lists, table, blocks, targets, total, sem
):
    loads = (
        pltpu.make_async_copy(blocks_in, blocks, sem.at[0]),
        pltpu.make_async_copy(table_in, table, sem.at[1]),
        pltpu.make_async_copy(lists_in, lists, sem.at[2]),
    )
    for load in loads:
        load.start()

    def clear(i, carry):
        for j in range(16):
            total[i * 16 + j] = jnp.zeros((16, RANK), F32)
        return carry

    lax.fori_loop(0, 4 * ROWS // 16, clear, 0)
    loads[0].wait()

    def spread(q, carry):
        for i in range(BLOCKS):
            block = blocks[q * BLOCKS + i]
            for j in range(8):
                start = pl.multiple_of(((q * BLOCKS + i) * 8 + j) * 128, 128)
                targets[pl.ds(start, 128), :] = block[:, 16 * j : 16 * j + 16]
        return carry

    lax.fori_loop(0, 4, spread, 0)
    loads[1].wait()
    loads[2].wait()

    end = 4 * ROWS - 1

    def step(carry):
        r, t, g = carry
        for _ in range(UNROLL):
            picked = [table[lists[r, 4 * g + i]] for i in range(4)]
            sources = jnp.concatenate([e[:, :RANK] for e in picked], axis=1)
            coefs = jnp.concatenate([e[:, RANK:] for e in picked], axis=1)
            mine = targets[pl.ds(pl.multiple_of(r * RANK, RANK), RANK), :]
            square = jnp.maximum(jnp.dot(mine, sources, preferred_element_type=F32), 1e-20)
            dist = square * lax.rsqrt(square)
            matrix = ((dist + 1.0 / SCALE) * jnp.exp2(dist * (-SCALE * LOG2E))).astype(BF16)
            total[r] += nt(coefs, matrix)
            done = g + 1 >= lists[r, 127]
            over = t == 72
            r = jnp.where(done, jnp.minimum(jnp.where(over, r + 8, r + 1), end), r)
            t = jnp.where(done, jnp.where(over, 0, t + 1), t)
            g = jnp.where(done, 0, g + 1)
        return r, t, g

    lax.while_loop(lambda c: c[0] < end, step, (jnp.int32(0), jnp.int32(0), jnp.int32(0)))

    def pack(q, carry):
        for i in range(PAIRS):
            at = q * ROWS + 2 * i
            both = jnp.concatenate([total[at], total[at + 1]], axis=1)
            out[q, i] = (both * (AMPLITUDE * SCALE)).astype(BF16)
        return carry

    lax.fori_loop(0, 4, pack, 0)


def coupling(lists, table, blocks):
    hbm = pl.BlockSpec(memory_space=pltpu.HBM)
    return pl.pallas_call(
        couple_kernel,
        in_specs=[hbm] * 3,
        out_specs=pl.BlockSpec(memory_space=pltpu.VMEM),
        scratch_shapes=[
            pltpu.SMEM((4 * ROWS, 128), jnp.int32),
            pltpu.VMEM((ENTRIES, 16, 128), BF16),
            pltpu.VMEM((4 * BLOCKS, 128, 128), BF16),
            pltpu.VMEM((4 * ROWS * RANK, 16), BF16),
            pltpu.VMEM((4 * ROWS, 16, RANK), F32),
            pltpu.SemaphoreType.DMA((3,)),
        ],
        out_shape=jax.ShapeDtypeStruct((4, PAIRS, 16, 128), BF16),
        compiler_params=pltpu.CompilerParams(vmem_limit_bytes=VMEM_BYTES),
        name="coupling",
    )(lists, table, blocks)


def down_kernel(
    far, basis_in, t_one_in, t_two_in, out, basis, t_one, t_two, came, near, in_sem, send, recv
):
    space = lax.axis_index("space")
    leaf = lax.axis_index("leaf")
    x = leaf // 4
    four = lax.rem(leaf, 4)
    barrier = pltpu.get_barrier_semaphore()
    for k in range(1, 4):
        to = lax.rem(x + k, 4) * 4 + four
        pl.semaphore_signal(barrier, inc=1, device_id=(space, to), device_id_type=MESH)
    loads = [
        pltpu.make_async_copy(src, dst, in_sem.at[k])
        for k, (src, dst) in enumerate(((far.at[x], came.at[x]), (t_two_in, t_two), (t_one_in, t_one), (basis_in, basis)))
    ]
    for load in loads:
        load.start()
    pl.semaphore_wait(barrier, 3)

    def copy(part, k):
        to = lax.rem(x + k, 4)
        pairs = pl.ds(*DOWN_PARTS[part])
        return pltpu.make_async_remote_copy(
            src_ref=far.at[to, pairs], dst_ref=came.at[x, pairs], send_sem=send.at[part, k],
            recv_sem=recv.at[part, x], device_id=(space, to * 4 + four), device_id_type=MESH,
        )

    def arrived(part):
        pairs = pl.ds(*DOWN_PARTS[part])
        for k in range(1, 4):
            source = lax.rem(x + k, 4)
            pltpu.make_async_remote_copy(
                src_ref=far.at[source, pairs], dst_ref=came.at[source, pairs], send_sem=send.at[part, k],
                recv_sem=recv.at[part, source], device_id=(space, leaf), device_id_type=MESH,
            ).wait_recv()

    for part in range(len(DOWN_PARTS)):
        for k in (2, 1, 3):
            copy(part, k).start()
    for load in loads:
        load.wait()
    arrived(0)

    def summed(i):
        return (
            came[0, i].astype(F32) + came[1, i].astype(F32)
            + came[2, i].astype(F32) + came[3, i].astype(F32)
        )

    local_two = summed(36)[:, :RANK].astype(BF16)
    down_one = jnp.dot(local_two, t_two[0], preferred_element_type=F32)
    for i in range(4):
        near[32 + i] = (summed(32 + i) + down_one[:, 128 * i : 128 * i + 128]).astype(BF16)

    def cluster(i, carry):
        both = near[32 + i]
        for h in range(2):
            local_one = both[:, h * RANK : (h + 1) * RANK]
            down_leaf = jnp.dot(local_one, t_one[2 * i + h], preferred_element_type=F32)
            for j in range(4):
                pair = 8 * i + 4 * h + j
                local_leaf = (summed(pair) + down_leaf[:, 128 * j : 128 * j + 128]).astype(BF16)
                for s in range(2):
                    at = pl.multiple_of((2 * pair + s) * 128, 128)
                    out[:, pl.ds(at, 128)] = jnp.dot(
                        local_leaf[:, s * RANK : (s + 1) * RANK], basis[2 * pair + s],
                        preferred_element_type=F32,
                    ).astype(BF16)
        return carry

    for part in range(1, len(DOWN_PARTS)):
        arrived(part)
        start, size = DOWN_PARTS[part]
        lax.fori_loop(start // 8, (start + size) // 8, cluster, 0)
    for part in range(len(DOWN_PARTS)):
        for k in range(1, 4):
            copy(part, k).wait_send()


def downward(far, basis, t_one, t_two):
    hbm = pl.BlockSpec(memory_space=pltpu.HBM)
    dma = pltpu.SemaphoreType.DMA
    return pl.pallas_call(
        down_kernel,
        out_shape=jax.ShapeDtypeStruct((16, LEAF_DEV * 128), BF16),
        in_specs=[hbm] * 4,
        out_specs=pl.BlockSpec(memory_space=pltpu.VMEM),
        scratch_shapes=[pltpu.VMEM(a.shape, a.dtype) for a in (basis, t_one, t_two)]
        + [
            pltpu.VMEM((4, PAIRS, 16, 128), BF16),
            pltpu.VMEM((36, 16, 128), BF16),
            dma((4,)), dma((len(DOWN_PARTS), 4)), dma((len(DOWN_PARTS), 4)),
        ],
        compiler_params=pltpu.CompilerParams(
            collective_id=1, has_side_effects=True, vmem_limit_bytes=DOWN_BYTES
        ),
        name="downward",
    )(far, basis, t_one, t_two)


def local(
    charges, leaf_basis, transfer_one, transfer_two, nodes_leaf, nodes_one, nodes_two,
    links_leaf, links_one, links_two,
):
    table, blocks, lists = upward(
        lax.axis_size("space"), charges, leaf_basis, transfer_one, transfer_two,
        nodes_leaf.transpose(1, 0, 2), nodes_one.transpose(1, 0, 2), nodes_two.reshape(3, RANK),
        links_leaf, links_one, links_two,
    )
    far = coupling(lists.reshape(4 * ROWS, 128), table, blocks)
    return downward(far, leaf_basis, transfer_one, transfer_two)


def solution(mesh):
    return jax.shard_map(
        local,
        mesh=mesh,
        in_specs=(
            P(None, ("space", "leaf")),
            P(("space", "leaf"), None, None),
            P(("space", "leaf"), None, None),
            P(("space", "leaf"), None, None),
            P(("space", "leaf"), None, None),
            P(("space", "leaf"), None, None),
            P(("space", "leaf"), None, None),
            P(("space", "leaf"), None),
            P(("space", "leaf"), None),
            P(("space", "leaf"), None),
        ),
        out_specs=P(None, ("space", "leaf")),
        check_vma=False,
    )
```
